256 devices in a mesh: group: 32 (over z, y), dom: 8 (over x, core).
Axes of the slice: x: 4, y: 4, z: 8, core: 2. Of those that a mesh axis runs over, the one named last changes fastest.
Arguments:
- blocks: bfloat16 [6656, 11, 128, 128], P(('group', 'dom')), may hold values from -0.5 to 0.5
- columns: int32 [6656, 11], P(('group', 'dom')), may hold values from 0 to 63, as said below
- sends: int32 [9728], P(('group', 'dom')), may hold values from 0 to 25, as said below
- active_row_count: int32 [256], P(('group', 'dom')), may hold values from 8 to 26, as said below
- degree: float32 [6656, 128], P(('group', 'dom')), may hold values from 1 to 16
- start: float32 [6656, 128, 128], P(('group', 'dom')), may hold values from -6 to 6
Outputs:
- basis: float32 [6656, 128, 128], P(('group', 'dom'))
- factor: float32 [128, 128], replicated
The draws below stay inside these ranges and needn't reach their ends.
Inputs may be any that keep to these rules, and one draw needn't show every extreme that they name: `active_row_count`: some device holds exactly 26 live slots in every draw; slots from the count on are dead. `columns`: position 0 of a slot is the slot itself; a live slot's other positions name live own slots or halo entries of the extended list, and every halo entry is named by some live slot. `sends`: each names a live slot of the sending device.
All inputs are finite; a program needn't handle non-finite values.
Results may differ from the reference program's by a relative error of at most 0.004.
Values may be sent and summed in bfloat16 or wider, within the bound.
No kernel may reach another device: no remote copies, remote signals or barrier semaphores. Data moves between devices by JAX's collectives and lax.ppermute only.
A program may use at most 128 MiB of HBM per device.

```python
import math
import jax
import jax.numpy as jnp
from jax import lax

BLOCK_NODES = 128
EIGEN_COUNT = 128
ROW_BLOCKS = 11
DEVICE_SLOTS = 26
ITERS = 2
HG = 13
HD = 6
NH = 38
TOTAL_SLOTS = 6656
N_GROUP = 32
N_DOM = 8


def live_counts(key):
    key = jax.random.fold_in(key, 11)
    first, second, third = jax.random.split(key, 3)
    device_list = N_GROUP * N_DOM
    lower = jax.random.randint(first, (device_list,), DEVICE_SLOTS // 3, DEVICE_SLOTS // 2 + 1)
    busy = jax.random.randint(second, (device_list,), 0, 8) == 0
    chosen = jax.random.randint(third, (), 0, device_list)
    counts = jnp.where(busy, DEVICE_SLOTS, lower)
    counts = jnp.where(jnp.arange(device_list) == chosen, DEVICE_SLOTS, counts)
    return counts.astype(jnp.int32)


def draw_active_row_count(key, part):
    return live_counts(key)


def draw_sends(key, part):
    counts = live_counts(key)
    key = jax.random.fold_in(key, 5)
    device_list = N_GROUP * N_DOM
    picked = jax.random.randint(key, (device_list, NH), 0, counts[:, None])
    return picked.reshape(device_list * NH).astype(jnp.int32)


def draw_columns(key, part):
    counts = live_counts(key)
    key = jax.random.fold_in(key, 7)
    first, second, third = jax.random.split(key, 3)
    device_list = N_GROUP * N_DOM
    shape = (device_list, DEVICE_SLOTS, ROW_BLOCKS)
    slot = jnp.arange(DEVICE_SLOTS, dtype=jnp.int32)[None, :, None]
    entry = jnp.arange(ROW_BLOCKS, dtype=jnp.int32)[None, None, :]
    position = slot * (ROW_BLOCKS - 1) + entry - 1
    covered = (entry >= 1) & (position < NH)
    own_pick = jax.random.randint(first, shape, 0, counts[:, None, None])
    halo_pick = DEVICE_SLOTS + jax.random.randint(second, shape, 0, NH)
    toward_halo = jax.random.randint(third, shape, 0, 2) == 0
    random_pick = jnp.where(toward_halo, halo_pick, own_pick)
    chosen = jnp.where(entry == 0, slot, jnp.where(covered, DEVICE_SLOTS + position, random_pick))
    chosen = jnp.broadcast_to(chosen, shape)
    return chosen.reshape(device_list * DEVICE_SLOTS, ROW_BLOCKS).astype(jnp.int32)


def levels(stream_key, extent, pieces, low, high):
    loudness, own = 1.0, jax.random.fold_in(stream_key, 6)
    for axis_at, shards_of in pieces:
        steps = jnp.exp(jax.random.uniform(jax.random.fold_in(own, axis_at), (shards_of,), jnp.float32, low / len(pieces), high / len(pieces)))
        loudness = loudness * jnp.repeat(steps, extent[axis_at] // shards_of).reshape([-1 if axis == axis_at else 1 for axis in range(len(extent))])
    return loudness


def normal_values(own_key, dims, width, limit, cuts=(), kind=jnp.bfloat16):
    factor_of = levels(own_key, dims, cuts, -0.22, 0.18) if cuts else 1.0
    values = jax.random.normal(own_key, dims, jnp.float32) * width * factor_of
    return jnp.minimum(jnp.maximum(values, -limit), limit).astype(kind)


def setup_inputs(seed: int = 0) -> dict:
    streams_of = jax.random.split(jax.random.key(seed), 7)
    blocks = normal_values(streams_of[0], (TOTAL_SLOTS, ROW_BLOCKS, BLOCK_NODES, BLOCK_NODES), (ROW_BLOCKS * 14) ** -0.5, 0.5, ((0, 256),))
    columns = draw_columns(jax.random.fold_in(streams_of[6], 71), 0)
    sends = draw_sends(jax.random.fold_in(streams_of[6], 71), 0)
    active_row_count = draw_active_row_count(jax.random.fold_in(streams_of[6], 71), 0)
    degree = jnp.clip(jnp.exp(math.log(16.0) - 2.7725887 * jax.random.uniform(streams_of[4], (TOTAL_SLOTS, BLOCK_NODES), jnp.float32) ** levels(streams_of[4], (TOTAL_SLOTS, BLOCK_NODES), ((0, 256),), -0.2, 0.2)), 1.0, 16.0)
    start = normal_values(streams_of[5], (TOTAL_SLOTS, BLOCK_NODES, EIGEN_COUNT), 1.0, 6.0, ((0, 256),), jnp.float32)
    return {"blocks": blocks, "columns": columns, "sends": sends, "active_row_count": active_row_count, "degree": degree, "start": start}


def reference(blocks, columns, sends, active_row_count, degree, start):
    device_list = N_GROUP * N_DOM
    upper_limit = lax.Precision.HIGHEST
    active_rows = (jnp.arange(DEVICE_SLOTS, dtype=jnp.int32)[None, :] < active_row_count[:, None]).reshape(TOTAL_SLOTS)
    scale = lax.rsqrt(degree)
    current = jnp.where(active_rows[:, None, None], start, jnp.float32(0.0))
    send_table = sends.reshape(device_list, NH)
    block_table = blocks.reshape(device_list, DEVICE_SLOTS, ROW_BLOCKS, BLOCK_NODES, BLOCK_NODES)
    column_table = columns.reshape(device_list, DEVICE_SLOTS, ROW_BLOCKS)
    factor = jnp.zeros((EIGEN_COUNT, EIGEN_COUNT), jnp.float32)
    for step in range(ITERS):
        operand = (scale[:, :, None] * current).astype(jnp.bfloat16)
        operand_dev = operand.reshape(device_list, DEVICE_SLOTS, BLOCK_NODES, EIGEN_COUNT)

        def single_device(dev):
            slab = dev // N_DOM
            place = dev % N_DOM
            below = (slab - 1) % N_GROUP * N_DOM + place
            above = (slab + 1) % N_GROUP * N_DOM + place
            left = slab * N_DOM + jnp.maximum(place - 1, 0)
            right = slab * N_DOM + jnp.minimum(place + 1, N_DOM - 1)

            def taken(src, low, count):
                return operand_dev[src][send_table[src][low:low + count]]
            part_below = taken(below, 0, HG)
            part_above = taken(above, HG, HG)
            part_left = jnp.where(place > 0, taken(left, 2 * HG, HD), jnp.zeros((HD, BLOCK_NODES, EIGEN_COUNT), jnp.bfloat16))
            part_right = jnp.where(place < N_DOM - 1, taken(right, 2 * HG + HD, HD), jnp.zeros((HD, BLOCK_NODES, EIGEN_COUNT), jnp.bfloat16))
            extended = jnp.concatenate([operand_dev[dev], part_below, part_above, part_left, part_right], axis=0)
            gathered = extended[column_table[dev]]
            return jnp.einsum('skij,skjc->sic', block_table[dev].astype(jnp.float32), gathered.astype(jnp.float32))
        matrix_product = lax.map(single_device, jnp.arange(device_list, dtype=jnp.int32)).reshape(TOTAL_SLOTS, BLOCK_NODES, EIGEN_COUNT)
        operator_image = jnp.where(active_rows[:, None, None], current + scale[:, :, None] * matrix_product, jnp.float32(0.0))
        gram_matrix = jnp.einsum('qhp,qhz->pz', operator_image, operator_image, precision=upper_limit) / jnp.float32(TOTAL_SLOTS * BLOCK_NODES)
        factor = jnp.linalg.cholesky(gram_matrix)
        inverse = jax.scipy.linalg.solve_triangular(factor, jnp.eye(EIGEN_COUNT, dtype=jnp.float32), lower=True)
        current = jnp.einsum('sic,dc->sid', operator_image, inverse, precision=upper_limit)
    return (current, factor)
```

```python
import functools
import jax
import jax.numpy as jnp
from jax import lax
from jax.experimental import pallas as pl
from jax.experimental.pallas import tpu as pltpu
from jax.sharding import PartitionSpec as P

AXES = ("group", "dom")
F32, BF16 = jnp.float32, jnp.bfloat16
VMEM_BYTES = 56 * 2**20
ANY = pl.BlockSpec(memory_space=pl.ANY)
SMEM = pl.BlockSpec(memory_space=pltpu.SMEM)
VMEM = pl.BlockSpec(memory_space=pltpu.VMEM)


def split3(x):
    high = x.astype(BF16)
    rest = x - high.astype(F32)
    mid = rest.astype(BF16)
    low = (rest - mid.astype(F32)).astype(BF16)
    return high, mid, low


def dot(a, b):
    return jnp.dot(a, b, preferred_element_type=F32)


def dot_rows(a, b):
    return lax.dot_general(a, b, (((0,), (0,)), ((), ())), preferred_element_type=F32)


def scale_columns(degree_ref, slot):
    row = lax.rsqrt(degree_ref[pl.ds(slot, 1), :])
    width = row.shape[1]
    return jnp.broadcast_to(row, (width, width)).T


def add_gram(image, wide_ref, side_ref):
    high, mid, low = split3(image)
    wide_ref[...] += dot_rows(high, jnp.concatenate([high, mid], axis=1))
    left = jnp.concatenate([high, mid * BF16(0.5)], axis=0)
    side_ref[...] += dot_rows(left, jnp.concatenate([low, mid], axis=0))


def finish_gram(wide_ref, side_ref):
    width = side_ref.shape[0]
    cross = wide_ref[:, width:] + side_ref[...]
    return wide_ref[:, :width] + (cross + cross.T)


def put_sends(out_refs, sends_ref, block_ref):
    base = 0
    for out_ref in out_refs:
        def put(j, carry, out_ref=out_ref, base=base):
            out_ref[j] = block_ref[sends_ref[base + j]]
            return carry
        lax.fori_loop(0, out_ref.shape[0], put, 0)
        base += out_ref.shape[0]


def prep_kernel(sends_ref, count_ref, degree_ref, start_ref, *refs):
    out_refs, operand_ref = refs[:4], refs[4]

    def scaled(s, carry):
        operand_ref[s] = (scale_columns(degree_ref, s) * start_ref[s]).astype(BF16)
        return carry
    lax.fori_loop(0, count_ref[0], scaled, 0)
    put_sends(out_refs, sends_ref, operand_ref)


def product_kernel(sending, columns_ref, sends_ref, count_ref, degree_ref, current_hbm,
                   blocks_hbm, halo0, halo1, halo2, halo3, image_ref, gram_ref, *refs):
    out_refs = refs[:4] if sending else ()
    (blocks_ref, ext_ref, current_ref, scale_ref, next_ref, wide_ref, side_ref,
     block_sems, halo_sems, current_sem) = refs[len(out_refs):]
    slots = image_ref.shape[0]
    per_row = blocks_ref.shape[1]
    count = count_ref[0]
    current_copy = pltpu.make_async_copy(current_hbm, current_ref, current_sem)
    current_copy.start()
    halo_copies, base = [], slots
    for i, halo in enumerate((halo0, halo1, halo2, halo3)):
        size = halo.shape[0]
        halo_copies.append(pltpu.make_async_copy(halo, ext_ref.at[pl.ds(base, size)], halo_sems.at[i]))
        halo_copies[-1].start()
        base += size

    def block_copy(s):
        return pltpu.make_async_copy(blocks_hbm.at[s], blocks_ref.at[s], block_sems.at[s])

    def begin(s, carry):
        block_copy(s).start()
        return carry
    lax.fori_loop(0, count, begin, 0)
    wide_ref[...] = jnp.zeros_like(wide_ref)
    side_ref[...] = jnp.zeros_like(side_ref)
    current_copy.wait()

    def own(s, carry):
        scale = scale_columns(degree_ref, s)
        scale_ref[s] = scale
        ext_ref[s] = (scale * current_ref[s]).astype(BF16)
        return carry
    lax.fori_loop(0, count, own, 0)
    for copy in halo_copies:
        copy.wait()

    def row(s, carry):
        block_copy(s).wait()
        left = jnp.concatenate([blocks_ref[s, k] for k in range(per_row)], axis=1)
        right = jnp.concatenate([ext_ref[columns_ref[s, k]] for k in range(per_row)], axis=0)
        scale = scale_ref[s]
        image = current_ref[s] + scale * dot(left, right)
        image_ref[s] = image
        add_gram(image, wide_ref, side_ref)
        if sending:
            next_ref[s] = (scale * image).astype(BF16)
        return carry
    lax.fori_loop(0, count, row, 0)

    def dead(s, carry):
        image_ref[s] = jnp.zeros(image_ref.shape[1:], F32)
        return carry
    lax.fori_loop(count, slots, dead, 0)
    gram_ref[...] = finish_gram(wide_ref, side_ref)
    if sending:
        put_sends(out_refs, sends_ref, next_ref)


def factorize(work_ref):
    size = work_ref.shape[0]
    step = 8
    sublane = lax.broadcasted_iota(jnp.int32, (step, size), 0)
    for top in range(0, size, step):
        rows = work_ref[top:top + step, :]
        main = [jnp.broadcast_to(rows[i:i + 1, :size], (step, size)) for i in range(step)]
        side = [jnp.broadcast_to(rows[i:i + 1, size:], (step, size)) for i in range(step)]
        entry = [[jnp.broadcast_to(main[i][:, top + k:top + k + 1], (step, size)) if k >= i else None
                  for k in range(step)] for i in range(step)]
        for j in range(step):
            inv = lax.rsqrt(entry[j][j])
            main[j] = main[j] * inv
            side[j] = side[j] * inv
            scaled = [entry[j][k] * inv if k > j else None for k in range(step)]
            for i in range(j + 1, step):
                for k in range(i, step):
                    entry[i][k] = entry[i][k] - scaled[i] * scaled[k]
                main[i] = main[i] - scaled[i] * main[j]
                side[i] = side[i] - scaled[i] * side[j]
        upper, inverse = main[0], side[0]
        for j in range(1, step):
            upper = jnp.where(sublane == j, main[j], upper)
            inverse = jnp.where(sublane == j, side[j], inverse)
        both = jnp.concatenate([upper, inverse], axis=1)
        work_ref[top:top + step, :] = both
        if top + step < size:
            h, m, l = split3(both)
            a, b, c = h[:, :size], m[:, :size], l[:, :size]
            left = jnp.concatenate([a, a, b, b, a, c], axis=0)
            right = jnp.concatenate([h, m, h, m, l, h], axis=0)
            update = dot_rows(left, right)
            work_ref[top + step:, :] -= update[top + step:, :]


def start_factor(gram, denominator, work_ref):
    size = work_ref.shape[0]
    rows = lax.broadcasted_iota(jnp.int32, (size, size), 0)
    columns = lax.broadcasted_iota(jnp.int32, (size, size), 1)
    work_ref[:, :size] = gram * F32(1.0 / denominator)
    work_ref[:, size:] = (rows == columns).astype(F32)
    factorize(work_ref)
    return rows, columns


def wide_weights(inverse, wide_ref):
    high, mid, _ = split3(inverse.T)
    half = jnp.concatenate([high, mid], axis=1)
    wide_ref[...] = jnp.concatenate([half, half], axis=0)


def times_weights(image, wide_ref):
    width = image.shape[1]
    high = image.astype(BF16)
    mid = (image - high.astype(F32)).astype(BF16)
    both = dot(jnp.concatenate([high, mid], axis=1), wide_ref[...])
    return both[:, :width] + both[:, width:]


def middle_kernel(denominator, parts, count_ref, *refs):
    gram_refs, image_hbm, image_ref, gram_ref = refs[:parts], refs[parts], refs[parts + 1], refs[parts + 2]
    work_ref, weights_ref, held_ref, wide_ref, side_ref, sem = refs[parts + 3:]
    count = count_ref[0]
    copy = pltpu.make_async_copy(image_hbm, held_ref, sem)
    copy.start()
    gram = functools.reduce(lambda a, b: a + b, [r[...] for r in gram_refs])
    start_factor(gram, denominator, work_ref)
    size = work_ref.shape[0]
    wide_weights(work_ref[:, size:], weights_ref)
    wide_ref[...] = jnp.zeros_like(wide_ref)
    side_ref[...] = jnp.zeros_like(side_ref)
    copy.wait()

    def row(s, carry):
        image = times_weights(held_ref[s], weights_ref)
        image_ref[s] = image
        add_gram(image, wide_ref, side_ref)
        return carry
    lax.fori_loop(0, count, row, 0)

    def dead(s, carry):
        image_ref[s] = jnp.zeros(image_ref.shape[1:], F32)
        return carry
    lax.fori_loop(count, image_ref.shape[0], dead, 0)
    gram_ref[...] = finish_gram(wide_ref, side_ref)


def last_kernel(denominator, parts, count_ref, *refs):
    gram_refs, image_hbm, basis_hbm, factor_ref = refs[:parts], refs[parts], refs[parts + 1], refs[parts + 2]
    work_ref, weights_ref, held_ref, basis_ref, sem, out_sems = refs[parts + 3:]
    slots = held_ref.shape[0]
    count = count_ref[0]
    copy = pltpu.make_async_copy(image_hbm, held_ref, sem)
    copy.start()
    gram = functools.reduce(lambda a, b: a + b, [r[...] for r in gram_refs])
    rows, columns = start_factor(gram, denominator, work_ref)
    size = work_ref.shape[0]
    wide_weights(work_ref[:, size:], weights_ref)
    copy.wait()

    def out_copy(s):
        return pltpu.make_async_copy(basis_ref.at[s], basis_hbm.at[s], out_sems.at[s])

    def row(s, carry):
        basis_ref[s] = times_weights(held_ref[s], weights_ref)
        out_copy(s).start()
        return carry
    lax.fori_loop(0, count, row, 0)

    def dead(s, carry):
        basis_ref[s] = jnp.zeros(basis_ref.shape[1:], F32)
        out_copy(s).start()
        return carry
    lax.fori_loop(count, slots, dead, 0)
    factor_ref[...] = jnp.where(rows <= columns, work_ref[:, :size], 0.0).T

    def finish(s, carry):
        out_copy(s).wait()
        return carry
    lax.fori_loop(0, slots, finish, 0)


def params():
    return pltpu.CompilerParams(vmem_limit_bytes=VMEM_BYTES)


def spread(shape_dtype):
    return jax.ShapeDtypeStruct(*shape_dtype)


def prep(sends, count, degree, start, sizes):
    slots, nodes, width = start.shape
    return pl.pallas_call(
        prep_kernel,
        out_shape=[spread(((n, nodes, width), BF16)) for n in sizes],
        in_specs=[SMEM, SMEM, VMEM, VMEM],
        out_specs=[VMEM] * 4,
        scratch_shapes=[pltpu.VMEM((slots, nodes, width), BF16)],
        compiler_params=params(),
        name="prep",
    )(sends, count, degree, start)


def product(columns, sends, count, degree, current, blocks, halos, sending):
    slots, nodes, width = current.shape
    sizes = [h.shape[0] for h in halos]
    out_shape = [spread((current.shape, F32)), spread(((width, width), F32))]
    if sending:
        out_shape += [spread(((n, nodes, width), BF16)) for n in sizes]
    return pl.pallas_call(
        functools.partial(product_kernel, sending),
        out_shape=out_shape,
        in_specs=[SMEM, SMEM, SMEM, VMEM] + [ANY] * 6,
        out_specs=[VMEM] * len(out_shape),
        scratch_shapes=[
            pltpu.VMEM(blocks.shape, BF16),
            pltpu.VMEM((slots + sum(sizes), nodes, width), BF16),
            pltpu.VMEM(current.shape, F32),
            pltpu.VMEM(current.shape, F32),
            pltpu.VMEM(current.shape, BF16),
            pltpu.VMEM((width, 2 * width), F32),
            pltpu.VMEM((width, width), F32),
            pltpu.SemaphoreType.DMA((slots,)),
            pltpu.SemaphoreType.DMA((4,)),
            pltpu.SemaphoreType.DMA(()),
        ],
        compiler_params=params(),
        name="product",
    )(columns, sends, count, degree, current, blocks, *halos)


def middle(parts, count, image, denominator):
    width = image.shape[2]
    return pl.pallas_call(
        functools.partial(middle_kernel, denominator, len(parts)),
        out_shape=[spread((image.shape, F32)), spread(((width, width), F32))],
        in_specs=[SMEM] + [VMEM] * len(parts) + [ANY],
        out_specs=[VMEM, VMEM],
        scratch_shapes=[
            pltpu.VMEM((width, 2 * width), F32),
            pltpu.VMEM((2 * width, 2 * width), BF16),
            pltpu.VMEM(image.shape, F32),
            pltpu.VMEM((width, 2 * width), F32),
            pltpu.VMEM((width, width), F32),
            pltpu.SemaphoreType.DMA(()),
        ],
        compiler_params=params(),
        name="middle",
    )(count, *parts, image)


def last(parts, count, image, denominator):
    width = image.shape[2]
    return pl.pallas_call(
        functools.partial(last_kernel, denominator, len(parts)),
        out_shape=[spread((image.shape, F32)), spread(((width, width), F32))],
        in_specs=[SMEM] + [VMEM] * len(parts) + [ANY],
        out_specs=[ANY, VMEM],
        scratch_shapes=[
            pltpu.VMEM((width, 2 * width), F32),
            pltpu.VMEM((2 * width, 2 * width), BF16),
            pltpu.VMEM(image.shape, F32),
            pltpu.VMEM(image.shape, F32),
            pltpu.SemaphoreType.DMA(()),
            pltpu.SemaphoreType.DMA((image.shape[0],)),
        ],
        compiler_params=params(),
        name="last",
    )(count, *parts, image)


def shift(shard, axis, by, wrap):
    size = lax.axis_size(axis)
    route = [(i, (i + by) % size) for i in range(size) if wrap or 0 <= i + by < size]
    return lax.ppermute(shard, axis, route)


def exchange(sent):
    to_next, to_prev, to_right, to_left = sent
    return (shift(to_next, "group", 1, True), shift(to_prev, "group", -1, True),
            shift(to_right, "dom", 1, False), shift(to_left, "dom", -1, False))


def swap(value, mask):
    size = lax.axis_size("group") * lax.axis_size("dom")
    return lax.ppermute(value, AXES, [(i, i ^ mask) for i in range(size)])


def sum_parts(value):
    size = lax.axis_size("group") * lax.axis_size("dom")
    masks = [1 << b for b in range(size.bit_length() - 1)]
    for mask in masks[:-1]:
        value = value + swap(value, mask)
    return [value, swap(value, masks[-1])]


def sum_gathered(gram):
    groups, parts = lax.axis_size("group"), lax.axis_size("dom")
    width = gram.shape[1]
    mine = lax.all_to_all(gram.reshape(parts, -1, width), "dom", 0, 0, tiled=True).sum(0)
    mine = lax.all_to_all(jnp.broadcast_to(mine, (groups,) + mine.shape), "group", 0, 0, tiled=True).sum(0)
    whole = lax.all_to_all(jnp.broadcast_to(mine, (parts,) + mine.shape), "dom", 0, 0, tiled=True)
    return [whole.reshape(gram.shape)]


def body(blocks, columns, sends, active_row_count, degree, start):
    slots, _, nodes, _ = blocks.shape
    denominator = lax.axis_size("group") * lax.axis_size("dom") * slots * nodes
    sizes = (slots // 2, slots // 2, slots // 4, slots // 4)
    halo = exchange(prep(sends, active_row_count, degree, start, sizes))
    image, gram, *sent = product(columns, sends, active_row_count, degree, start, blocks, halo, True)
    halo = exchange(sent)
    parts = sum_parts(gram)
    image, _ = product(columns, sends, active_row_count, degree, image, blocks, halo, False)
    image, gram = middle(parts, active_row_count, image, denominator)
    return tuple(last(sum_gathered(gram), active_row_count, image, denominator))


def solution(mesh):
    return jax.shard_map(
        body,
        mesh=mesh,
        in_specs=(
            P(AXES, None, None, None),
            P(AXES, None),
            P(AXES),
            P(AXES),
            P(AXES, None),
            P(AXES, None, None),
        ),
        out_specs=(P(AXES, None, None), P()),
        check_vma=False,
    )
```

```python
import functools
import jax
import jax.numpy as jnp
from jax import lax
from jax.experimental import pallas as pl
from jax.experimental.pallas import tpu as pltpu
from jax.sharding import PartitionSpec as P

AXES = ("group", "dom")
F32, BF16 = jnp.float32, jnp.bfloat16
PANEL = 16
ANY = pl.BlockSpec(memory_space=pl.ANY)
SMEM = pl.BlockSpec(memory_space=pltpu.SMEM)
VMEM = pl.BlockSpec(memory_space=pltpu.VMEM)


def split3(x):
    high = x.astype(BF16)
    rest = x - high.astype(F32)
    mid = rest.astype(BF16)
    low = (rest - mid.astype(F32)).astype(BF16)
    return high, mid, low


def dot(a, b):
    return jnp.dot(a, b, preferred_element_type=F32)


def dot_rows(a, b):
    return lax.dot_general(a, b, (((0,), (0,)), ((), ())), preferred_element_type=F32)


def scale_blocks(degree_ref):
    scale = lax.rsqrt(degree_ref[...])
    slots, nodes = scale.shape
    turned = jnp.concatenate([scale, jnp.zeros((nodes - slots, nodes), F32)], axis=0).T
    return [jnp.broadcast_to(turned[:, s:s + 1], (nodes, nodes)) for s in range(slots)]


def add_gram(parts, wide_ref, side_ref):
    high, mid, low = parts
    wide_ref[...] += dot_rows(high, jnp.concatenate([high, mid], axis=1))
    left = jnp.concatenate([high, mid * BF16(0.5)], axis=0)
    side_ref[...] += dot_rows(left, jnp.concatenate([low, mid], axis=0))


def finish_gram(wide_ref, side_ref):
    width = side_ref.shape[0]
    cross = wide_ref[:, width:] + side_ref[...]
    return wide_ref[:, :width] + (cross + cross.T)


def put_sends(out_refs, sends_ref, block_ref):
    base = 0
    for out_ref in out_refs:
        for j in range(out_ref.shape[0]):
            out_ref[j] = block_ref[sends_ref[base + j]]
        base += out_ref.shape[0]


def prep_kernel(sends_ref, degree_ref, start_ref, operand_ref, *out_refs):
    for s, scale in enumerate(scale_blocks(degree_ref)):
        operand_ref[s] = (scale * start_ref[s]).astype(BF16)
    put_sends(out_refs, sends_ref, operand_ref)


def load_kernel(blocks_hbm, after_ref, blocks_ref, sem):
    copy = pltpu.make_async_copy(blocks_hbm, blocks_ref, sem)
    copy.start()
    copy.wait()


def product_kernel(sending, columns_ref, sends_ref, count_ref, degree_ref, current_ref, operand_ref,
                   blocks_ref, halo0, halo1, halo2, halo3, image_ref, gram_ref, *refs):
    next_ref, out_refs = (refs[0], refs[1:5]) if sending else (None, ())
    ext_ref, scale_ref, parts_ref, wide_ref, side_ref = refs[1 + len(out_refs) if sending else 0:]
    slots, per_row = blocks_ref.shape[:2]
    group = parts_ref.shape[1] // image_ref.shape[1]
    count = count_ref[0]
    base = 0
    for piece in (operand_ref, halo0, halo1, halo2, halo3):
        size = piece.shape[0]
        ext_ref[base:base + size] = piece[...]
        base += size
    wide_ref[...] = jnp.zeros_like(wide_ref)
    side_ref[...] = jnp.zeros_like(side_ref)
    parts_ref[...] = jnp.zeros_like(parts_ref)
    for s, scale in enumerate(scale_blocks(degree_ref)):
        scale_ref[s] = scale

    def row(s):
        left = jnp.concatenate([blocks_ref[s, k] for k in range(per_row)], axis=1)
        right = jnp.concatenate([ext_ref[columns_ref[k, s]] for k in range(per_row)], axis=0)
        image = current_ref[s] + scale_ref[s] * dot(left, right)
        return jnp.where(s < count, image, 0.0)

    def rows(step, carry):
        add_gram([parts_ref[i] for i in range(3)], wide_ref, side_ref)
        first = step * group
        images = [row(first + i) for i in range(group)]
        for i, image in enumerate(images):
            image_ref[first + i] = image
            if sending:
                next_ref[first + i] = (scale_ref[first + i] * image).astype(BF16)
        for i, part in enumerate(split3(jnp.concatenate(images, axis=0))):
            parts_ref[i] = part
        return carry
    steps = (count + group - 1) // group
    lax.fori_loop(0, steps, rows, 0)
    add_gram([parts_ref[i] for i in range(3)], wide_ref, side_ref)

    def dead(s, carry):
        image_ref[s] = jnp.zeros(image_ref.shape[1:], F32)
        return carry
    lax.fori_loop(steps * group, slots, dead, 0)
    gram_ref[...] = finish_gram(wide_ref, side_ref)
    if sending:
        put_sends(out_refs, sends_ref, next_ref)


def gather_rows(rows, sublane):
    lanes = sublane.shape[0]
    pieces = []
    for first in range(0, len(rows), lanes):
        piece = rows[first]
        for j in range(1, lanes):
            piece = jnp.where(sublane == j, rows[first + j], piece)
        pieces.append(piece)
    return jnp.concatenate(pieces, axis=0)


def factorize(work_ref):
    size = work_ref.shape[0]
    step, lanes = PANEL, 8
    sublane = lax.broadcasted_iota(jnp.int32, (lanes, size), 0)
    for top in range(0, size, step):
        rows = work_ref[top:top + step, :]
        main = [jnp.broadcast_to(rows[i:i + 1, :size], (lanes, size)) for i in range(step)]
        side = [jnp.broadcast_to(rows[i:i + 1, size:], (lanes, size)) for i in range(step)]
        entry = [[jnp.broadcast_to(main[i][:, top + k:top + k + 1], (lanes, size)) if k >= i else None
                  for k in range(step)] for i in range(step)]
        for j in range(step):
            inv = lax.rsqrt(entry[j][j])
            main[j] = main[j] * inv
            side[j] = side[j] * inv
            scaled = [entry[j][k] * inv if k > j else None for k in range(step)]
            for i in range(j + 1, step):
                for k in range(i, step):
                    entry[i][k] = entry[i][k] - scaled[i] * scaled[k]
                main[i] = main[i] - scaled[i] * main[j]
                side[i] = side[i] - scaled[i] * side[j]
        both = jnp.concatenate([gather_rows(main, sublane), gather_rows(side, sublane)], axis=1)
        work_ref[top:top + step, :] = both
        if top + step < size:
            h, m, l = split3(both)
            a, b, c = h[:, :size], m[:, :size], l[:, :size]
            left = jnp.concatenate([a, a, b, b, a, c], axis=0)
            right = jnp.concatenate([h, m, h, m, l, h], axis=0)
            update = dot_rows(left, right)
            work_ref[top + step:, :] -= update[top + step:, :]


def start_factor(gram, denominator, work_ref):
    size = work_ref.shape[0]
    rows = lax.broadcasted_iota(jnp.int32, (size, size), 0)
    columns = lax.broadcasted_iota(jnp.int32, (size, size), 1)
    work_ref[:, :size] = gram * F32(1.0 / denominator)
    work_ref[:, size:] = (rows == columns).astype(F32)
    factorize(work_ref)
    return rows, columns


def dot_full(a, b):
    ah, am, al = split3(a)
    bh, bm, bl = split3(b)
    left = jnp.concatenate([ah, ah, am, ah, am, al], axis=1)
    right = jnp.concatenate([bh, bm, bh, bl, bm, bh], axis=0)
    return dot(left, right)


def wide_weights(weights, wide_ref):
    high, mid, _ = split3(weights)
    half = jnp.concatenate([high, mid], axis=1)
    wide_ref[...] = jnp.concatenate([half, half], axis=0)


def times_weights(image, wide_ref):
    width = image.shape[1]
    high = image.astype(BF16)
    mid = (image - high.astype(F32)).astype(BF16)
    both = dot(jnp.concatenate([high, mid], axis=1), wide_ref[...])
    return both[:, :width] + both[:, width:]


def last_kernel(denominator, grams_ref, image_ref, basis_hbm, factor_ref,
                work_ref, weights_ref, basis_ref, out_sems):
    slots, nodes, width = image_ref.shape
    start_factor(grams_ref[0], denominator, work_ref)
    first = work_ref[:, width:]
    turned = first.T
    rows, columns = start_factor(dot_full(dot_full(first, grams_ref[1]), turned), denominator, work_ref)
    wide_weights(dot_full(turned, work_ref[:, width:].T), weights_ref)
    half = slots // 2

    def out_copy(part):
        chunk = pl.ds(part * half, half)
        return pltpu.make_async_copy(basis_ref.at[chunk], basis_hbm.at[chunk], out_sems.at[part])

    def apply(s, carry):
        basis_ref[s] = times_weights(image_ref[s], weights_ref)
        return carry
    for part in range(2):
        lax.fori_loop(part * half, (part + 1) * half, apply, 0, unroll=half)
        out_copy(part).start()
    factor_ref[...] = jnp.where(rows <= columns, work_ref[:, :width], 0.0).T
    for part in range(2):
        out_copy(part).wait()


def params(limit):
    return pltpu.CompilerParams(vmem_limit_bytes=limit * 2**20)


def spread(shape, dtype):
    return jax.ShapeDtypeStruct(shape, dtype)


def prep(sends, degree, start, sizes):
    slots, nodes, width = start.shape
    return pl.pallas_call(
        prep_kernel,
        out_shape=[spread((n, nodes, width), BF16) for n in (slots,) + sizes],
        in_specs=[SMEM, VMEM, VMEM],
        out_specs=[VMEM] * 5,
        compiler_params=params(16),
        name="prep",
    )(sends, degree, start)


def load(blocks, after):
    size = blocks.size * blocks.dtype.itemsize
    return pl.pallas_call(
        load_kernel,
        out_shape=spread(blocks.shape, blocks.dtype),
        in_specs=[ANY, ANY],
        out_specs=VMEM,
        scratch_shapes=[pltpu.SemaphoreType.DMA(())],
        compiler_params=params(40),
        cost_estimate=pl.CostEstimate(flops=0, bytes_accessed=2 * size, transcendentals=0),
        name="load",
    )(blocks, after)


def product(columns, sends, count, degree, current, operand, blocks, halos, sending):
    slots, nodes, width = current.shape
    sizes = [h.shape[0] for h in halos]
    out_shape = [spread(current.shape, F32), spread((width, width), F32)]
    if sending:
        out_shape += [spread((n, nodes, width), BF16) for n in [slots] + sizes]
    group = 2
    return pl.pallas_call(
        functools.partial(product_kernel, sending),
        out_shape=out_shape,
        in_specs=[SMEM] * 3 + [VMEM] * 8,
        out_specs=[VMEM] * len(out_shape),
        scratch_shapes=[
            pltpu.VMEM((slots + sum(sizes), nodes, width), BF16),
            pltpu.VMEM(current.shape, F32),
            pltpu.VMEM((3, group * nodes, width), BF16),
            pltpu.VMEM((width, 2 * width), F32),
            pltpu.VMEM((width, width), F32),
        ],
        compiler_params=params(28),
        name="product",
    )(columns, sends, count, degree, current, operand, blocks, *halos)


def last(grams, image, denominator):
    slots, nodes, width = image.shape
    return pl.pallas_call(
        functools.partial(last_kernel, denominator),
        out_shape=[spread(image.shape, F32), spread((width, width), F32)],
        in_specs=[VMEM, VMEM],
        out_specs=[ANY, VMEM],
        scratch_shapes=[
            pltpu.VMEM((width, 2 * width), F32),
            pltpu.VMEM((2 * width, 2 * width), BF16),
            pltpu.VMEM(image.shape, F32),
            pltpu.SemaphoreType.DMA((2,)),
        ],
        compiler_params=params(16),
        name="last",
    )(grams, image)


def shift(shard, axis, by, wrap):
    size = lax.axis_size(axis)
    route = [(i, (i + by) % size) for i in range(size) if wrap or 0 <= i + by < size]
    return lax.ppermute(shard, axis, route)


def exchange(sent):
    to_next, to_prev, to_right, to_left = sent
    return (shift(to_next, "group", 1, True), shift(to_prev, "group", -1, True),
            shift(to_right, "dom", 1, False), shift(to_left, "dom", -1, False))


def collected(value, axis):
    size = lax.axis_size(axis)
    return lax.all_to_all(jnp.broadcast_to(value, (size,) + value.shape), axis, 0, 0, tiled=True)


def summed(grams):
    count, rows, width = grams.shape
    parts = lax.axis_size("dom")
    pieces = grams.reshape(count, parts, rows // parts, width).transpose(1, 0, 2, 3)
    mine = lax.all_to_all(pieces, "dom", 0, 0, tiled=True).sum(0)
    mine = collected(mine, "group").sum(0)
    whole = collected(mine, "dom")
    return whole.transpose(1, 0, 2, 3).reshape(grams.shape)


def body(blocks, columns, sends, active_row_count, degree, start):
    slots, _, nodes, _ = blocks.shape
    denominator = lax.axis_size("group") * lax.axis_size("dom") * slots * nodes
    sizes = (slots // 2, slots // 2, slots // 4, slots // 4)
    table = (columns.T, sends, active_row_count, degree)
    operand, *sent = prep(sends, degree, start, sizes)
    blocks = load(blocks, operand)
    image, first_gram, operand, *sent = product(*table, start, operand, blocks, exchange(sent), True)
    image, gram = product(*table, image, operand, blocks, exchange(sent), False)
    grams = summed(jnp.stack([first_gram, gram]))
    return last(grams, image, denominator)


def solution(mesh):
    return jax.shard_map(
        body,
        mesh=mesh,
        in_specs=(
            P(AXES, None, None, None),
            P(AXES, None),
            P(AXES),
            P(AXES),
            P(AXES, None),
            P(AXES, None, None),
        ),
        out_specs=(P(AXES, None, None), P()),
        check_vma=False,
    )
```

```python
import functools
import jax
import jax.numpy as jnp
from jax import lax
from jax.experimental import pallas as pl
from jax.experimental.pallas import tpu as pltpu
from jax.sharding import PartitionSpec as P

AXES = ("group", "dom")
F32, BF16 = jnp.float32, jnp.bfloat16
PANEL = 16
ANY = pl.BlockSpec(memory_space=pl.ANY)
SMEM = pl.BlockSpec(memory_space=pltpu.SMEM)
VMEM = pl.BlockSpec(memory_space=pltpu.VMEM)


def split3(x):
    high = x.astype(BF16)
    rest = x - high.astype(F32)
    mid = rest.astype(BF16)
    low = (rest - mid.astype(F32)).astype(BF16)
    return high, mid, low


def dot(a, b):
    return jnp.dot(a, b, preferred_element_type=F32)


def dot_rows(a, b):
    return lax.dot_general(a, b, (((0,), (0,)), ((), ())), preferred_element_type=F32)


def scale_blocks(degree_ref):
    scale = lax.rsqrt(degree_ref[...])
    slots, nodes = scale.shape
    turned = jnp.concatenate([scale, jnp.zeros((nodes - slots, nodes), F32)], axis=0).T
    return [jnp.broadcast_to(turned[:, s:s + 1], (nodes, nodes)) for s in range(slots)]


def add_gram(parts, wide_ref, side_ref):
    high, mid, low = parts
    wide_ref[...] += dot_rows(high, jnp.concatenate([high, mid], axis=1))
    left = jnp.concatenate([high, mid * BF16(0.5)], axis=0)
    side_ref[...] += dot_rows(left, jnp.concatenate([low, mid], axis=0))


def finish_gram(wide_ref, side_ref):
    width = side_ref.shape[0]
    cross = wide_ref[:, width:] + side_ref[...]
    return wide_ref[:, :width] + (cross + cross.T)


def pack_gram(gram):
    half, quarter = gram.shape[0] // 2, gram.shape[0] // 4
    left = lax.broadcasted_iota(jnp.int32, (half, gram.shape[1]), 1) < half
    low = gram[half:]
    blocks = jnp.where(left, gram[:half], low)
    corner = jnp.where(left[:quarter], low[:quarter], pltpu.roll(low[quarter:], half, 1))
    return jnp.concatenate([blocks, corner], axis=0)


def unpack_gram(packed):
    size = packed.shape[1]
    half = size // 2
    left = lax.broadcasted_iota(jnp.int32, (half, size), 1) < half
    corner = jnp.concatenate([packed[half:], pltpu.roll(packed[half:], half, 1)], axis=0)
    low = jnp.where(left, corner, packed[:half])
    full = jnp.concatenate([packed[:half], low], axis=0)
    rows = lax.broadcasted_iota(jnp.int32, (size, size), 0)
    columns = lax.broadcasted_iota(jnp.int32, (size, size), 1)
    return jnp.where(rows > columns, full, 0.0) + jnp.where(rows >= columns, full, 0.0).T


def put_sends(out_refs, sends_ref, block_ref):
    base = 0
    for out_ref in out_refs:
        for j in range(out_ref.shape[0]):
            out_ref[j] = block_ref[sends_ref[base + j]]
        base += out_ref.shape[0]


def prep_kernel(sends_hbm, degree_hbm, start_hbm, token_ref, operand_ref, *refs):
    out_refs = refs[:4]
    sends_ref, degree_ref, start_ref, sems = refs[4:]
    half = start_ref.shape[0] // 2
    halves = [pl.ds(0, half), pl.ds(half, half)]
    copies = [pltpu.make_async_copy(degree_hbm, degree_ref, sems.at[0])]
    copies += [pltpu.make_async_copy(start_hbm.at[part], start_ref.at[part], sems.at[1 + i])
               for i, part in enumerate(halves)]
    copies += [pltpu.make_async_copy(sends_hbm, sends_ref, sems.at[3])]
    for copy in copies:
        copy.start()
    token_ref[...] = jnp.zeros_like(token_ref)
    copies[0].wait()
    for s, scale in enumerate(scale_blocks(degree_ref)):
        if s % half == 0:
            copies[1 + s // half].wait()
        operand_ref[s] = (scale * start_ref[s]).astype(BF16)
    copies[3].wait()
    put_sends(out_refs, sends_ref, operand_ref)


def load_kernel(blocks_hbm, after_ref, blocks_ref, sem):
    copy = pltpu.make_async_copy(blocks_hbm, blocks_ref, sem)
    copy.start()
    copy.wait()


def product_kernel(sending, columns_ref, sends_ref, count_ref, degree_ref, current_ref, operand_ref,
                   blocks_ref, halo0, halo1, halo2, halo3, other_ref, image_ref, gram_ref, *refs):
    next_ref, out_refs = (refs[0], refs[1:5]) if sending else (None, ())
    ext_ref, scale_ref, parts_ref, wide_ref, side_ref = refs[1 + len(out_refs) if sending else 0:]
    slots, per_row = blocks_ref.shape[:2]
    group = parts_ref.shape[1] // image_ref.shape[1]
    count = count_ref[0]
    base = 0
    for piece in (operand_ref, halo0, halo1, halo2, halo3):
        size = piece.shape[0]
        ext_ref[base:base + size] = piece[...]
        base += size
    wide_ref[...] = jnp.zeros_like(wide_ref)
    side_ref[...] = jnp.zeros_like(side_ref)
    parts_ref[...] = jnp.zeros_like(parts_ref)
    for s, scale in enumerate(scale_blocks(degree_ref)):
        scale_ref[s] = scale

    def row(s):
        left = jnp.concatenate([blocks_ref[s, k] for k in range(per_row)], axis=1)
        right = jnp.concatenate([ext_ref[columns_ref[k, s]] for k in range(per_row)], axis=0)
        image = current_ref[s] + scale_ref[s] * dot(left, right)
        return jnp.where(s < count, image, 0.0)

    def rows(step, carry):
        add_gram([parts_ref[i] for i in range(3)], wide_ref, side_ref)
        first = step * group
        images = [row(first + i) for i in range(group)]
        for i, image in enumerate(images):
            image_ref[first + i] = image
            if sending:
                next_ref[first + i] = (scale_ref[first + i] * image).astype(BF16)
        for i, part in enumerate(split3(jnp.concatenate(images, axis=0))):
            parts_ref[i] = part
        return carry
    steps = (count + group - 1) // group
    lax.fori_loop(0, steps, rows, 0)
    add_gram([parts_ref[i] for i in range(3)], wide_ref, side_ref)

    def dead(s, carry):
        image_ref[s] = jnp.zeros(image_ref.shape[1:], F32)
        return carry
    lax.fori_loop(steps * group, slots, dead, 0)
    gram = pack_gram(finish_gram(wide_ref, side_ref))
    gram_ref[...] = gram if sending else jnp.concatenate([other_ref[...], gram], axis=0)
    if sending:
        put_sends(out_refs, sends_ref, next_ref)


def gather_rows(rows, sublane):
    lanes = sublane.shape[0]
    pieces = []
    for first in range(0, len(rows), lanes):
        piece = rows[first]
        for j in range(1, lanes):
            piece = jnp.where(sublane == j, rows[first + j], piece)
        pieces.append(piece)
    return jnp.concatenate(pieces, axis=0)


def factorize(work_ref):
    size = work_ref.shape[0]
    step, lanes = PANEL, 8
    sublane = lax.broadcasted_iota(jnp.int32, (lanes, size), 0)
    for top in range(0, size, step):
        rows = work_ref[top:top + step, :]
        main = [jnp.broadcast_to(rows[i:i + 1, :size], (lanes, size)) for i in range(step)]
        side = [jnp.broadcast_to(rows[i:i + 1, size:], (lanes, size)) for i in range(step)]
        entry = [[jnp.broadcast_to(main[i][:, top + k:top + k + 1], (lanes, size)) if k >= i else None
                  for k in range(step)] for i in range(step)]
        for j in range(step):
            inv = lax.rsqrt(entry[j][j])
            main[j] = main[j] * inv
            side[j] = side[j] * inv
            scaled = [entry[j][k] * inv if k > j else None for k in range(step)]
            for i in range(j + 1, step):
                for k in range(i, step):
                    entry[i][k] = entry[i][k] - scaled[i] * scaled[k]
                main[i] = main[i] - scaled[i] * main[j]
                side[i] = side[i] - scaled[i] * side[j]
        both = jnp.concatenate([gather_rows(main, sublane), gather_rows(side, sublane)], axis=1)
        work_ref[top:top + step, :] = both
        if top + step < size:
            h, m, l = split3(both)
            a, b, c = h[:, :size], m[:, :size], l[:, :size]
            left = jnp.concatenate([a, a, b, b, a, c], axis=0)
            right = jnp.concatenate([h, m, h, m, l, h], axis=0)
            update = dot_rows(left, right)
            work_ref[top + step:, :] -= update[top + step:, :]


def start_factor(gram, denominator, work_ref):
    size = work_ref.shape[0]
    rows = lax.broadcasted_iota(jnp.int32, (size, size), 0)
    columns = lax.broadcasted_iota(jnp.int32, (size, size), 1)
    work_ref[:, :size] = gram * F32(1.0 / denominator)
    work_ref[:, size:] = (rows == columns).astype(F32)
    factorize(work_ref)
    return rows, columns


def dot_full(a, b):
    ah, am, al = split3(a)
    bh, bm, bl = split3(b)
    left = jnp.concatenate([ah, ah, am, ah, am, al], axis=1)
    right = jnp.concatenate([bh, bm, bh, bl, bm, bh], axis=0)
    return dot(left, right)


def wide_weights(weights, wide_ref):
    high, mid, _ = split3(weights)
    half = jnp.concatenate([high, mid], axis=1)
    wide_ref[...] = jnp.concatenate([half, half], axis=0)


def times_weights(image, wide_ref):
    width = image.shape[1]
    high = image.astype(BF16)
    mid = (image - high.astype(F32)).astype(BF16)
    both = dot(jnp.concatenate([high, mid], axis=1), wide_ref[...])
    return both[:, :width] + both[:, width:]


def last_kernel(denominator, grams_ref, image_ref, basis_hbm, factor_ref,
                work_ref, weights_ref, basis_ref, out_sems):
    slots, nodes, width = image_ref.shape
    half_rows = grams_ref.shape[0] // 2
    start_factor(unpack_gram(grams_ref[:half_rows]), denominator, work_ref)
    first = work_ref[:, width:]
    turned = first.T
    second = dot_full(dot_full(first, unpack_gram(grams_ref[half_rows:])), turned)
    rows, columns = start_factor(second, denominator, work_ref)
    wide_weights(dot_full(turned, work_ref[:, width:].T), weights_ref)
    half = slots // 2

    def out_copy(part):
        chunk = pl.ds(part * half, half)
        return pltpu.make_async_copy(basis_ref.at[chunk], basis_hbm.at[chunk], out_sems.at[part])

    def apply(s, carry):
        basis_ref[s] = times_weights(image_ref[s], weights_ref)
        return carry
    for part in range(2):
        lax.fori_loop(part * half, (part + 1) * half, apply, 0, unroll=half)
        out_copy(part).start()
    factor_ref[...] = jnp.where(rows <= columns, work_ref[:, :width], 0.0).T
    for part in range(2):
        out_copy(part).wait()


def params(limit):
    return pltpu.CompilerParams(vmem_limit_bytes=limit * 2**20)


def spread(shape, dtype):
    return jax.ShapeDtypeStruct(shape, dtype)


def prep(sends, degree, start, sizes):
    slots, nodes, width = start.shape
    return pl.pallas_call(
        prep_kernel,
        out_shape=[spread((8, width), F32)] + [spread((n, nodes, width), BF16) for n in (slots,) + sizes],
        in_specs=[ANY] * 3,
        out_specs=[VMEM] * 6,
        scratch_shapes=[
            pltpu.SMEM(sends.shape, sends.dtype),
            pltpu.VMEM(degree.shape, F32),
            pltpu.VMEM(start.shape, F32),
            pltpu.SemaphoreType.DMA((4,)),
        ],
        compiler_params=params(58),
        name="prep",
    )(sends, degree, start)


def load(blocks, after):
    size = blocks.size * blocks.dtype.itemsize
    return pl.pallas_call(
        load_kernel,
        out_shape=spread(blocks.shape, blocks.dtype),
        in_specs=[ANY, ANY],
        out_specs=VMEM,
        scratch_shapes=[pltpu.SemaphoreType.DMA(())],
        compiler_params=params(40),
        cost_estimate=pl.CostEstimate(flops=0, bytes_accessed=2 * size, transcendentals=0),
        name="load",
    )(blocks, after)


def product(columns, sends, count, degree, current, operand, blocks, halos, other):
    slots, nodes, width = current.shape
    sizes = [h.shape[0] for h in halos]
    sending = other is None
    rows = 3 * width // 4
    out_shape = [spread(current.shape, F32), spread((rows if sending else 2 * rows, width), F32)]
    if sending:
        out_shape += [spread((n, nodes, width), BF16) for n in [slots] + sizes]
    group = 2
    return pl.pallas_call(
        functools.partial(product_kernel, sending),
        out_shape=out_shape,
        in_specs=[SMEM] * 3 + [VMEM] * 9,
        out_specs=[VMEM] * len(out_shape),
        scratch_shapes=[
            pltpu.VMEM((slots + sum(sizes), nodes, width), BF16),
            pltpu.VMEM(current.shape, F32),
            pltpu.VMEM((3, group * nodes, width), BF16),
            pltpu.VMEM((width, 2 * width), F32),
            pltpu.VMEM((width, width), F32),
        ],
        compiler_params=params(28),
        name="product",
    )(columns, sends, count, degree, current, operand, blocks, *halos, degree if sending else other)


def last(grams, image, denominator):
    slots, nodes, width = image.shape
    return pl.pallas_call(
        functools.partial(last_kernel, denominator),
        out_shape=[spread(image.shape, F32), spread((width, width), F32)],
        in_specs=[VMEM, VMEM],
        out_specs=[ANY, VMEM],
        scratch_shapes=[
            pltpu.VMEM((width, 2 * width), F32),
            pltpu.VMEM((2 * width, 2 * width), BF16),
            pltpu.VMEM(image.shape, F32),
            pltpu.SemaphoreType.DMA((2,)),
        ],
        compiler_params=params(16),
        name="last",
    )(grams, image)


def shift(shard, axis, by, wrap):
    size = lax.axis_size(axis)
    route = [(i, (i + by) % size) for i in range(size) if wrap or 0 <= i + by < size]
    return lax.ppermute(shard, axis, route)


def exchange(sent):
    to_next, to_prev, to_right, to_left = sent
    return (shift(to_next, "group", 1, True), shift(to_prev, "group", -1, True),
            shift(to_right, "dom", 1, False), shift(to_left, "dom", -1, False))


def collected(value, axis):
    size = lax.axis_size(axis)
    return lax.all_to_all(jnp.broadcast_to(value, (size,) + value.shape), axis, 0, 0, tiled=True)


def summed(grams):
    pieces = grams.reshape(lax.axis_size("dom"), -1, grams.shape[1])
    mine = lax.all_to_all(pieces, "dom", 0, 0, tiled=True).sum(0)
    mine = collected(mine, "group").sum(0)
    return collected(mine, "dom").reshape(grams.shape)


def body(blocks, columns, sends, active_row_count, degree, start):
    slots, _, nodes, _ = blocks.shape
    denominator = lax.axis_size("group") * lax.axis_size("dom") * slots * nodes
    sizes = (slots // 2, slots // 2, slots // 4, slots // 4)
    table = (columns.T, sends, active_row_count, degree)
    token, operand, *sent = prep(sends, degree, start, sizes)
    blocks = load(blocks, token)
    image, first_gram, operand, *sent = product(*table, start, operand, blocks, exchange(sent), None)
    image, grams = product(*table, image, operand, blocks, exchange(sent), first_gram)
    return last(summed(grams), image, denominator)


def solution(mesh):
    return jax.shard_map(
        body,
        mesh=mesh,
        in_specs=(
            P(AXES, None, None, None),
            P(AXES, None),
            P(AXES),
            P(AXES),
            P(AXES, None),
            P(AXES, None, None),
        ),
        out_specs=(P(AXES, None, None), P()),
        check_vma=False,
    )
```

```python
import functools
import math
import jax
import jax.numpy as jnp
from jax import lax
from jax.experimental import pallas as pl
from jax.experimental.pallas import tpu as pltpu
from jax.sharding import PartitionSpec as P

AXES = ("group", "dom")
F32, BF16 = jnp.float32, jnp.bfloat16
PANEL = 16
LIMIT1 = 36
ANY = pl.BlockSpec(memory_space=pl.ANY)
SMEM = pl.BlockSpec(memory_space=pltpu.SMEM)
VMEM = pl.BlockSpec(memory_space=pltpu.VMEM)


def split3(x):
    high = x.astype(BF16)
    rest = x - high.astype(F32)
    mid = rest.astype(BF16)
    low = (rest - mid.astype(F32)).astype(BF16)
    return high, mid, low


def dot(a, b):
    return jnp.dot(a, b, preferred_element_type=F32)


def dot_rows(a, b):
    return lax.dot_general(a, b, (((0,), (0,)), ((), ())), preferred_element_type=F32)


def scale_blocks(degree_ref):
    scale = lax.rsqrt(degree_ref[...])
    slots, nodes = scale.shape
    turned = jnp.concatenate([scale, jnp.zeros((nodes - slots, nodes), F32)], axis=0).T
    return [jnp.broadcast_to(turned[:, s:s + 1], (nodes, nodes)) for s in range(slots)]


def add_gram(parts, wide_ref, side_ref):
    high, mid, low = parts
    wide_ref[...] += dot_rows(high, jnp.concatenate([high, mid], axis=1))
    left = jnp.concatenate([high, mid * BF16(0.5)], axis=0)
    side_ref[...] += dot_rows(left, jnp.concatenate([low, mid], axis=0))


def finish_gram(wide_ref, side_ref):
    width = side_ref.shape[0]
    cross = wide_ref[:, width:] + side_ref[...]
    return wide_ref[:, :width] + (cross + cross.T)


def pack_gram(gram):
    half, quarter = gram.shape[0] // 2, gram.shape[0] // 4
    left = lax.broadcasted_iota(jnp.int32, (half, gram.shape[1]), 1) < half
    low = gram[half:]
    blocks = jnp.where(left, gram[:half], low)
    corner = jnp.where(left[:quarter], low[:quarter], pltpu.roll(low[quarter:], half, 1))
    return jnp.concatenate([blocks, corner], axis=0)


def unpack_gram(packed):
    size = packed.shape[1]
    half = size // 2
    left = lax.broadcasted_iota(jnp.int32, (half, size), 1) < half
    corner = jnp.concatenate([packed[half:], pltpu.roll(packed[half:], half, 1)], axis=0)
    low = jnp.where(left, corner, packed[:half])
    full = jnp.concatenate([packed[:half], low], axis=0)
    rows = lax.broadcasted_iota(jnp.int32, (size, size), 0)
    columns = lax.broadcasted_iota(jnp.int32, (size, size), 1)
    return jnp.where(rows > columns, full, 0.0) + jnp.where(rows >= columns, full, 0.0).T


def put_sends(out_refs, sends_ref, block_ref):
    base = 0
    for out_ref in out_refs:
        for j in range(out_ref.shape[0]):
            out_ref[j] = block_ref[sends_ref[base + j]]
        base += out_ref.shape[0]


def prep_kernel(sends_hbm, degree_hbm, start_hbm, *refs):
    out_refs = refs[:4]
    operand_ref, sends_ref, degree_ref, start_ref, sems = refs[4:]
    half = start_ref.shape[0] // 2
    halves = [pl.ds(0, half), pl.ds(half, half)]
    copies = [pltpu.make_async_copy(degree_hbm, degree_ref, sems.at[0])]
    copies += [pltpu.make_async_copy(start_hbm.at[part], start_ref.at[part], sems.at[1 + i])
               for i, part in enumerate(halves)]
    copies += [pltpu.make_async_copy(sends_hbm, sends_ref, sems.at[3])]
    for copy in copies:
        copy.start()
    copies[0].wait()
    for s, scale in enumerate(scale_blocks(degree_ref)):
        if s % half == 0:
            copies[1 + s // half].wait()
        operand_ref[s] = (scale * start_ref[s]).astype(BF16)
    copies[3].wait()
    put_sends(out_refs, sends_ref, operand_ref)


def chunk_bounds(slots, group):
    steps = slots // group
    return sorted({0, steps // 6, steps // 3, 2 * steps // 3, steps})


def product_kernel(sending, columns_ref, sends_ref, count_ref, core_ref, degree_ref, current_ref,
                   blocks_hbm, halo0, halo1, halo2, halo3, *refs):
    ext_ref, scale_ref, next_ref, parts_ref, wide_ref, side_ref, sems = refs[-7:]
    if sending:
        image_ref, gram_ref, blocks_ref, *out_refs = refs[:-7]
    else:
        other_ref, image_ref, mine_ref, yours_ref = refs[:-7]
        blocks_ref = blocks_hbm
    slots, per_row = blocks_ref.shape[:2]
    group = parts_ref.shape[1] // image_ref.shape[1]
    count = count_ref[0]
    bounds = chunk_bounds(slots, group)
    copies = []
    if sending:
        for i, (low, high) in enumerate(zip(bounds, bounds[1:])):
            chunk = pl.ds(low * group, (high - low) * group)
            copies.append(pltpu.make_async_copy(blocks_hbm.at[chunk], blocks_ref.at[chunk], sems.at[i]))
            copies[-1].start()
    for s, scale in enumerate(scale_blocks(degree_ref)):
        scale_ref[s] = scale
        ext_ref[s] = (scale * current_ref[s]).astype(BF16)
    base = slots
    for piece in (halo0, halo1, halo2, halo3):
        size = piece.shape[0]
        ext_ref[base:base + size] = piece[...]
        base += size
    wide_ref[...] = jnp.zeros_like(wide_ref)
    side_ref[...] = jnp.zeros_like(side_ref)
    parts_ref[...] = jnp.zeros_like(parts_ref)

    def row(s):
        left = jnp.concatenate([blocks_ref[s, k] for k in range(per_row)], axis=1)
        right = jnp.concatenate([ext_ref[columns_ref[k, s]] for k in range(per_row)], axis=0)
        image = current_ref[s] + scale_ref[s] * dot(left, right)
        return jnp.where(s < count, image, 0.0)

    def rows(step, carry):
        add_gram([parts_ref[i] for i in range(3)], wide_ref, side_ref)
        first = step * group
        images = [row(first + i) for i in range(group)]
        for i, image in enumerate(images):
            image_ref[first + i] = image
            if sending:
                next_ref[first + i] = (scale_ref[first + i] * image).astype(BF16)
        for i, part in enumerate(split3(jnp.concatenate(images, axis=0))):
            parts_ref[i] = part
        return carry
    steps = (count + group - 1) // group
    for i, (low, high) in enumerate(zip(bounds, bounds[1:])):
        if sending:
            copies[i].wait()
        lax.fori_loop(low, jnp.minimum(high, steps), rows, 0)
    add_gram([parts_ref[i] for i in range(3)], wide_ref, side_ref)

    def dead(s, carry):
        image_ref[s] = jnp.zeros(image_ref.shape[1:], F32)
        return carry
    lax.fori_loop(steps * group, slots, dead, 0)
    gram = pack_gram(finish_gram(wide_ref, side_ref))
    if sending:
        gram_ref[...] = gram
        put_sends(out_refs, sends_ref, next_ref)
    else:
        other, low_core = other_ref[...], core_ref[0] == 0
        mine_ref[...] = jnp.where(low_core, other, gram)
        yours_ref[...] = jnp.where(low_core, gram, other)


def gather_rows(rows, sublane):
    lanes = sublane.shape[0]
    pieces = []
    for first in range(0, len(rows), lanes):
        piece = rows[first]
        for j in range(1, lanes):
            piece = jnp.where(sublane == j, rows[first + j], piece)
        pieces.append(piece)
    return jnp.concatenate(pieces, axis=0)


def factorize(work_ref):
    size = work_ref.shape[0]
    step, lanes = PANEL, 8
    sublane = lax.broadcasted_iota(jnp.int32, (lanes, size), 0)
    for top in range(0, size, step):
        rows = work_ref[top:top + step, :]
        main = [jnp.broadcast_to(rows[i:i + 1, :size], (lanes, size)) for i in range(step)]
        side = [jnp.broadcast_to(rows[i:i + 1, size:], (lanes, size)) for i in range(step)]
        entry = [[jnp.broadcast_to(main[i][:, top + k:top + k + 1], (lanes, size)) if k >= i else None
                  for k in range(step)] for i in range(step)]
        for j in range(step):
            inv = lax.rsqrt(entry[j][j])
            main[j] = main[j] * inv
            side[j] = side[j] * inv
            scaled = [entry[j][k] * inv if k > j else None for k in range(step)]
            for i in range(j + 1, step):
                for k in range(i, step):
                    entry[i][k] = entry[i][k] - scaled[i] * scaled[k]
                main[i] = main[i] - scaled[i] * main[j]
                side[i] = side[i] - scaled[i] * side[j]
        both = jnp.concatenate([gather_rows(main, sublane), gather_rows(side, sublane)], axis=1)
        work_ref[top:top + step, :] = both
        if top + step < size:
            h, m, l = split3(both)
            a, b, c = h[:, :size], m[:, :size], l[:, :size]
            left = jnp.concatenate([a, a, b, b, a, c], axis=0)
            right = jnp.concatenate([h, m, h, m, l, h], axis=0)
            update = dot_rows(left, right)
            work_ref[top + step:, :] -= update[top + step:, :]


def start_factor(gram, denominator, work_ref):
    size = work_ref.shape[0]
    rows = lax.broadcasted_iota(jnp.int32, (size, size), 0)
    columns = lax.broadcasted_iota(jnp.int32, (size, size), 1)
    work_ref[:, :size] = gram * F32(1.0 / denominator)
    work_ref[:, size:] = (rows == columns).astype(F32)
    factorize(work_ref)
    return rows, columns


def dot_full(a, b):
    ah, am, al = split3(a)
    bh, bm, bl = split3(b)
    left = jnp.concatenate([ah, ah, am, ah, am, al], axis=1)
    right = jnp.concatenate([bh, bm, bh, bl, bm, bh], axis=0)
    return dot(left, right)


def wide_weights(weights, wide_ref):
    high, mid, _ = split3(weights)
    half = jnp.concatenate([high, mid], axis=1)
    wide_ref[...] = jnp.concatenate([half, half], axis=0)


def times_weights(image, wide_ref):
    width = image.shape[1]
    high = image.astype(BF16)
    mid = (image - high.astype(F32)).astype(BF16)
    both = dot(jnp.concatenate([high, mid], axis=1), wide_ref[...])
    return both[:, :width] + both[:, width:]


def last_kernel(denominator, core_ref, mine_ref, yours_ref, image_ref, basis_hbm, factor_ref,
                work_ref, weights_ref, basis_ref, out_sems):
    slots, nodes, width = image_ref.shape
    low_core = core_ref[0] == 0
    mine, yours = mine_ref[...], yours_ref[...]
    start_factor(unpack_gram(jnp.where(low_core, mine, yours)), denominator, work_ref)
    first = work_ref[:, width:]
    turned = first.T
    second = dot_full(dot_full(first, unpack_gram(jnp.where(low_core, yours, mine))), turned)
    rows, columns = start_factor(second, denominator, work_ref)
    wide_weights(dot_full(turned, work_ref[:, width:].T), weights_ref)
    half = slots // 2

    def out_copy(part):
        chunk = pl.ds(part * half, half)
        return pltpu.make_async_copy(basis_ref.at[chunk], basis_hbm.at[chunk], out_sems.at[part])

    def apply(s, carry):
        basis_ref[s] = times_weights(image_ref[s], weights_ref)
        return carry
    for part in range(2):
        lax.fori_loop(part * half, (part + 1) * half, apply, 0, unroll=half)
        out_copy(part).start()
    factor_ref[...] = jnp.where(rows <= columns, work_ref[:, :width], 0.0).T
    for part in range(2):
        out_copy(part).wait()


def params(limit):
    return pltpu.CompilerParams(vmem_limit_bytes=limit * 2**20)


def spread(shape, dtype):
    return jax.ShapeDtypeStruct(shape, dtype)


def prep(sends, degree, start, sizes):
    slots, nodes, width = start.shape
    return pl.pallas_call(
        prep_kernel,
        out_shape=[spread((n, nodes, width), BF16) for n in sizes],
        in_specs=[ANY] * 3,
        out_specs=[VMEM] * 4,
        scratch_shapes=[
            pltpu.VMEM(start.shape, BF16),
            pltpu.SMEM(sends.shape, sends.dtype),
            pltpu.VMEM(degree.shape, F32),
            pltpu.VMEM(start.shape, F32),
            pltpu.SemaphoreType.DMA((4,)),
        ],
        compiler_params=params(58),
        name="prep",
    )(sends, degree, start)


def product(columns, sends, count, core, degree, current, blocks, halos, other):
    slots, nodes, width = current.shape
    sizes = [h.shape[0] for h in halos]
    sending = other is None
    group = 2
    packed = spread((3 * width // 4, width), F32)
    out_shape = [spread(current.shape, F32), packed]
    if sending:
        out_shape += [spread(blocks.shape, BF16)]
        out_shape += [spread(h.shape, BF16) for h in halos]
    else:
        out_shape += [packed]
    return pl.pallas_call(
        functools.partial(product_kernel, sending),
        out_shape=out_shape,
        in_specs=[SMEM] * 4 + [VMEM] * 2 + [ANY if sending else VMEM] + [VMEM] * (4 if sending else 5),
        out_specs=[VMEM] * len(out_shape),
        scratch_shapes=[
            pltpu.VMEM((slots + sum(sizes), nodes, width), BF16),
            pltpu.VMEM(current.shape, F32),
            pltpu.VMEM(current.shape if sending else (1, 16, width), BF16),
            pltpu.VMEM((3, group * nodes, width), BF16),
            pltpu.VMEM((width, 2 * width), F32),
            pltpu.VMEM((width, width), F32),
            pltpu.SemaphoreType.DMA((len(chunk_bounds(slots, group)),)),
        ],
        compiler_params=params(LIMIT1 if sending else 28),
        name="product",
    )(columns, sends, count, core, degree, current, blocks, *halos, *([] if sending else [other]))


def last(core, mine, yours, image, denominator):
    slots, nodes, width = image.shape
    return pl.pallas_call(
        functools.partial(last_kernel, denominator),
        out_shape=[spread(image.shape, F32), spread((width, width), F32)],
        in_specs=[SMEM, VMEM, VMEM, VMEM],
        out_specs=[ANY, VMEM],
        scratch_shapes=[
            pltpu.VMEM((width, 2 * width), F32),
            pltpu.VMEM((2 * width, 2 * width), BF16),
            pltpu.VMEM(image.shape, F32),
            pltpu.SemaphoreType.DMA((2,)),
        ],
        compiler_params=params(16),
        name="last",
    )(core, mine, yours, image)


def shift(shard, axis, by, wrap):
    size = lax.axis_size(axis)
    route = [(i, (i + by) % size) for i in range(size) if wrap or 0 <= i + by < size]
    return lax.ppermute(shard, axis, route)


def exchange(sent):
    to_next, to_prev, to_right, to_left = sent
    return (shift(to_next, "group", 1, True), shift(to_prev, "group", -1, True),
            shift(to_right, "dom", 1, False), shift(to_left, "dom", -1, False))


def place():
    groups, parts = lax.axis_size("group"), lax.axis_size("dom")
    y = min(groups, 4)
    return groups // y, y, parts // 2, 2


def neighbours(value, dim, by):
    extents = place()
    size = math.prod(extents)
    stride = math.prod(extents[dim + 1:])
    route = []
    for i in range(size):
        at = i // stride % extents[dim]
        route.append((i, i + ((at + by) % extents[dim] - at) * stride))
    return lax.ppermute(value, AXES, route)


def sum_ring(value, dim):
    extent = place()[dim]
    order = sorted(range(1, extent), key=lambda k: min(k, extent - k))
    for piece in [neighbours(value, dim, k) for k in order]:
        value = value + piece
    return value


def sum_far(value):
    extents = place()
    depth, stride = extents[0], math.prod(extents[1:])
    if depth == 1:
        return value
    groups = [[z * stride + i for z in range(depth)] for i in range(stride)]
    copies = jnp.broadcast_to(value, (depth,) + value.shape)
    return lax.all_to_all(copies, AXES, 0, 0, axis_index_groups=groups, tiled=True).sum(0)


def summed(mine, yours):
    value = mine + neighbours(yours, 3, 1)
    value = sum_ring(value, 2)
    value = sum_ring(value, 1)
    value = sum_far(value)
    return value, neighbours(value, 3, 1)


def body(blocks, columns, sends, active_row_count, degree, start):
    slots, _, nodes, _ = blocks.shape
    denominator = lax.axis_size("group") * lax.axis_size("dom") * slots * nodes
    sizes = (slots // 2, slots // 2, slots // 4, slots // 4)
    core = lax.rem(lax.axis_index("dom"), 2).reshape(1)
    table = (columns.T, sends, active_row_count, core, degree)
    sent = prep(sends, degree, start, sizes)
    image, first_gram, blocks, *sent = product(*table, start, blocks, exchange(sent), None)
    image, mine, yours = product(*table, image, blocks, exchange(sent), first_gram)
    return last(core, *summed(mine, yours), image, denominator)


def solution(mesh):
    return jax.shard_map(
        body,
        mesh=mesh,
        in_specs=(
            P(AXES, None, None, None),
            P(AXES, None),
            P(AXES),
            P(AXES),
            P(AXES, None),
            P(AXES, None, None),
        ),
        out_specs=(P(AXES, None, None), P()),
        check_vma=False,
    )
```

```python
import functools
import math
import jax
import jax.numpy as jnp
from jax import lax
from jax.experimental import pallas as pl
from jax.experimental.pallas import tpu as pltpu
from jax.sharding import PartitionSpec as P

AXES = ("group", "dom")
F32, BF16 = jnp.float32, jnp.bfloat16
PANEL, GROUP = 16, 2
ANY = pl.BlockSpec(memory_space=pl.ANY)
SMEM = pl.BlockSpec(memory_space=pltpu.SMEM)
VMEM = pl.BlockSpec(memory_space=pltpu.VMEM)


def split3(x):
    high = x.astype(BF16)
    rest = x - high.astype(F32)
    mid = rest.astype(BF16)
    low = (rest - mid.astype(F32)).astype(BF16)
    return high, mid, low


def dot(a, b):
    return jnp.dot(a, b, preferred_element_type=F32)


def dot_rows(a, b):
    return lax.dot_general(a, b, (((0,), (0,)), ((), ())), preferred_element_type=F32)


def scale_blocks(degree_ref):
    scale = lax.rsqrt(degree_ref[...])
    slots, nodes = scale.shape
    turned = jnp.concatenate([scale, jnp.zeros((nodes - slots, nodes), F32)], axis=0).T
    return [jnp.broadcast_to(turned[:, s:s + 1], (nodes, nodes)) for s in range(slots)]


def add_gram(parts, wide_ref, side_ref):
    high, mid, low = parts
    wide_ref[...] += dot_rows(high, jnp.concatenate([high, mid], axis=1))
    left = jnp.concatenate([high, mid * BF16(0.5)], axis=0)
    side_ref[...] += dot_rows(left, jnp.concatenate([low, mid], axis=0))


def finish_gram(wide_ref, side_ref):
    width = side_ref.shape[0]
    cross = wide_ref[:, width:] + side_ref[...]
    return wide_ref[:, :width] + (cross + cross.T)


def pack_gram(gram):
    half, quarter = gram.shape[0] // 2, gram.shape[0] // 4
    left = lax.broadcasted_iota(jnp.int32, (half, gram.shape[1]), 1) < half
    low = gram[half:]
    blocks = jnp.where(left, gram[:half], low)
    corner = jnp.where(left[:quarter], low[:quarter], pltpu.roll(low[quarter:], half, 1))
    return jnp.concatenate([blocks, corner], axis=0)


def unpack_gram(packed):
    size = packed.shape[1]
    half = size // 2
    left = lax.broadcasted_iota(jnp.int32, (half, size), 1) < half
    corner = jnp.concatenate([packed[half:], pltpu.roll(packed[half:], half, 1)], axis=0)
    low = jnp.where(left, corner, packed[:half])
    full = jnp.concatenate([packed[:half], low], axis=0)
    rows = lax.broadcasted_iota(jnp.int32, (size, size), 0)
    columns = lax.broadcasted_iota(jnp.int32, (size, size), 1)
    return jnp.where(rows > columns, full, 0.0) + jnp.where(rows >= columns, full, 0.0).T


def put_sends(out_refs, sends_ref, block_ref):
    base = 0
    for out_ref in out_refs:
        for j in range(out_ref.shape[0]):
            out_ref[j] = block_ref[sends_ref[base + j]]
        base += out_ref.shape[0]


def prep_kernel(sends_hbm, degree_hbm, start_hbm, *refs):
    out_refs = refs[:4]
    operand_ref, sends_ref, degree_ref, start_ref, sems = refs[4:]
    half = start_ref.shape[0] // 2
    halves = [pl.ds(0, half), pl.ds(half, half)]
    copies = [pltpu.make_async_copy(degree_hbm, degree_ref, sems.at[0])]
    copies += [pltpu.make_async_copy(start_hbm.at[part], start_ref.at[part], sems.at[1 + i])
               for i, part in enumerate(halves)]
    copies += [pltpu.make_async_copy(sends_hbm, sends_ref, sems.at[3])]
    for copy in copies:
        copy.start()
    copies[0].wait()
    for s, scale in enumerate(scale_blocks(degree_ref)):
        if s % half == 0:
            copies[1 + s // half].wait()
        operand_ref[s] = (scale * start_ref[s]).astype(BF16)
    copies[3].wait()
    put_sends(out_refs, sends_ref, operand_ref)


def hold_kernel(blocks_hbm, degree_ref, blocks_ref, scale_ref, sem):
    copy = pltpu.make_async_copy(blocks_hbm, blocks_ref, sem)
    copy.start()
    for s, scale in enumerate(scale_blocks(degree_ref)):
        scale_ref[s] = scale
    copy.wait()


def product_kernel(sending, columns_ref, sends_ref, count_ref, core_ref, scale_ref, current_ref,
                   blocks_ref, halo0, halo1, halo2, halo3, *refs):
    if sending:
        image_ref, *out_refs, ext_ref, next_ref = refs
    else:
        other_ref, image_ref, mine_ref, yours_ref, ext_ref, parts_ref, wide_ref, side_ref = refs
    slots, per_row = blocks_ref.shape[:2]
    count = count_ref[0]
    for s in range(slots):
        ext_ref[s] = (scale_ref[s] * current_ref[s]).astype(BF16)
    base = slots
    for piece in (halo0, halo1, halo2, halo3):
        size = piece.shape[0]
        ext_ref[base:base + size] = piece[...]
        base += size
    if not sending:
        wide_ref[...] = jnp.zeros_like(wide_ref)
        side_ref[...] = jnp.zeros_like(side_ref)
        parts_ref[...] = jnp.zeros_like(parts_ref)

    def row(s):
        left = jnp.concatenate([blocks_ref[s, k] for k in range(per_row)], axis=1)
        right = jnp.concatenate([ext_ref[columns_ref[k, s]] for k in range(per_row)], axis=0)
        image = current_ref[s] + scale_ref[s] * dot(left, right)
        return jnp.where(s < count, image, 0.0)

    def rows(step, carry):
        if not sending:
            add_gram([parts_ref[i] for i in range(3)], wide_ref, side_ref)
        first = step * GROUP
        images = [row(first + i) for i in range(GROUP)]
        for i, image in enumerate(images):
            image_ref[first + i] = image
            if sending:
                next_ref[first + i] = (scale_ref[first + i] * image).astype(BF16)
        if not sending:
            for i, part in enumerate(split3(jnp.concatenate(images, axis=0))):
                parts_ref[i] = part
        return carry
    steps = (count + GROUP - 1) // GROUP
    lax.fori_loop(0, steps, rows, 0)

    def dead(s, carry):
        image_ref[s] = jnp.zeros(image_ref.shape[1:], F32)
        return carry
    lax.fori_loop(steps * GROUP, slots, dead, 0)
    if sending:
        put_sends(out_refs, sends_ref, next_ref)
    else:
        add_gram([parts_ref[i] for i in range(3)], wide_ref, side_ref)
        gram = pack_gram(finish_gram(wide_ref, side_ref))
        other, low_core = other_ref[...], core_ref[0] == 0
        mine_ref[...] = jnp.where(low_core, other, gram)
        yours_ref[...] = jnp.where(low_core, gram, other)


def gram_kernel(count_ref, image_ref, gram_ref, wide_ref, side_ref):
    wide_ref[...] = jnp.zeros_like(wide_ref)
    side_ref[...] = jnp.zeros_like(side_ref)

    def rows(step, carry):
        images = [image_ref[step * GROUP + i] for i in range(GROUP)]
        add_gram(split3(jnp.concatenate(images, axis=0)), wide_ref, side_ref)
        return carry
    lax.fori_loop(0, (count_ref[0] + GROUP - 1) // GROUP, rows, 0)
    gram_ref[...] = pack_gram(finish_gram(wide_ref, side_ref))


def gather_rows(rows, sublane):
    lanes = sublane.shape[0]
    pieces = []
    for first in range(0, len(rows), lanes):
        piece = rows[first]
        for j in range(1, lanes):
            piece = jnp.where(sublane == j, rows[first + j], piece)
        pieces.append(piece)
    return jnp.concatenate(pieces, axis=0)


def factorize(work_ref):
    size = work_ref.shape[0]
    step, lanes = PANEL, 8
    sublane = lax.broadcasted_iota(jnp.int32, (lanes, size), 0)
    for top in range(0, size, step):
        rows = work_ref[top:top + step, :]
        main = [jnp.broadcast_to(rows[i:i + 1, :size], (lanes, size)) for i in range(step)]
        side = [jnp.broadcast_to(rows[i:i + 1, size:], (lanes, size)) for i in range(step)]
        entry = [[jnp.broadcast_to(main[i][:, top + k:top + k + 1], (lanes, size)) if k >= i else None
                  for k in range(step)] for i in range(step)]
        for j in range(step):
            inv = lax.rsqrt(entry[j][j])
            main[j] = main[j] * inv
            side[j] = side[j] * inv
            scaled = [entry[j][k] * inv if k > j else None for k in range(step)]
            for i in range(j + 1, step):
                for k in range(i, step):
                    entry[i][k] = entry[i][k] - scaled[i] * scaled[k]
                main[i] = main[i] - scaled[i] * main[j]
                side[i] = side[i] - scaled[i] * side[j]
        both = jnp.concatenate([gather_rows(main, sublane), gather_rows(side, sublane)], axis=1)
        work_ref[top:top + step, :] = both
        if top + step < size:
            h, m, l = split3(both)
            a, b, c = h[:, :size], m[:, :size], l[:, :size]
            left = jnp.concatenate([a, a, b, b, a, c], axis=0)
            right = jnp.concatenate([h, m, h, m, l, h], axis=0)
            update = dot_rows(left, right)
            work_ref[top + step:, :] -= update[top + step:, :]


def start_factor(gram, denominator, work_ref):
    size = work_ref.shape[0]
    rows = lax.broadcasted_iota(jnp.int32, (size, size), 0)
    columns = lax.broadcasted_iota(jnp.int32, (size, size), 1)
    work_ref[:, :size] = gram * F32(1.0 / denominator)
    work_ref[:, size:] = (rows == columns).astype(F32)
    factorize(work_ref)
    return rows, columns


def dot_full(a, b):
    ah, am, al = split3(a)
    bh, bm, bl = split3(b)
    left = jnp.concatenate([ah, ah, am, ah, am, al], axis=1)
    right = jnp.concatenate([bh, bm, bh, bl, bm, bh], axis=0)
    return dot(left, right)


def wide_weights(weights, wide_ref):
    high, mid, _ = split3(weights)
    half = jnp.concatenate([high, mid], axis=1)
    wide_ref[...] = jnp.concatenate([half, half], axis=0)


def times_weights(image, wide_ref):
    width = image.shape[1]
    high = image.astype(BF16)
    mid = (image - high.astype(F32)).astype(BF16)
    both = dot(jnp.concatenate([high, mid], axis=1), wide_ref[...])
    return both[:, :width] + both[:, width:]


def factor_kernel(denominator, gram_ref, work_ref):
    start_factor(unpack_gram(gram_ref[...]), denominator, work_ref)


def last_kernel(core_ref, mine_ref, yours_ref, image_ref, basis_hbm, factor_ref,
                weights_ref, basis_ref, out_sems):
    slots, nodes, width = image_ref.shape
    low_core = core_ref[0] == 0
    both = jnp.where(low_core, yours_ref[...], mine_ref[...])
    first = jnp.where(low_core, mine_ref[:, width:], yours_ref[:, width:])
    wide_weights(both[:, width:].T, weights_ref)
    half = slots // 2

    def out_copy(part):
        chunk = pl.ds(part * half, half)
        return pltpu.make_async_copy(basis_ref.at[chunk], basis_hbm.at[chunk], out_sems.at[part])

    def apply(s, carry):
        basis_ref[s] = times_weights(image_ref[s], weights_ref)
        return carry
    for part in range(2):
        lax.fori_loop(part * half, (part + 1) * half, apply, 0, unroll=half)
        out_copy(part).start()
    rows = lax.broadcasted_iota(jnp.int32, (width, width), 0)
    columns = lax.broadcasted_iota(jnp.int32, (width, width), 1)
    joint = jnp.where(rows <= columns, both[:, :width], 0.0).T
    factor_ref[...] = jnp.where(rows >= columns, dot_full(first, joint), 0.0)
    for part in range(2):
        out_copy(part).wait()


def params(limit):
    return pltpu.CompilerParams(vmem_limit_bytes=limit * 2**20)


def spread(shape, dtype):
    return jax.ShapeDtypeStruct(shape, dtype)


def prep(sends, degree, start, sizes):
    slots, nodes, width = start.shape
    return pl.pallas_call(
        prep_kernel,
        out_shape=[spread((n, nodes, width), BF16) for n in sizes],
        in_specs=[ANY] * 3,
        out_specs=[VMEM] * 4,
        scratch_shapes=[
            pltpu.VMEM(start.shape, BF16),
            pltpu.SMEM(sends.shape, sends.dtype),
            pltpu.VMEM(degree.shape, F32),
            pltpu.VMEM(start.shape, F32),
            pltpu.SemaphoreType.DMA((4,)),
        ],
        compiler_params=params(58),
        name="prep",
    )(sends, degree, start)


def hold(blocks, degree, slots, nodes):
    size = blocks.size * blocks.dtype.itemsize
    return pl.pallas_call(
        hold_kernel,
        out_shape=[spread(blocks.shape, BF16), spread((slots, nodes, nodes), F32)],
        in_specs=[ANY, VMEM],
        out_specs=[VMEM, VMEM],
        scratch_shapes=[pltpu.SemaphoreType.DMA(())],
        compiler_params=params(36),
        cost_estimate=pl.CostEstimate(flops=0, bytes_accessed=2 * size, transcendentals=0),
        name="hold",
    )(blocks, degree)


def product(columns, sends, count, core, scale, current, blocks, halos, other):
    slots, nodes, width = current.shape
    sizes = [h.shape[0] for h in halos]
    sending = other is None
    packed = spread((3 * width // 4, width), F32)
    scratch = [pltpu.VMEM((slots + sum(sizes), nodes, width), BF16)]
    if sending:
        out_shape = [spread(h.shape, BF16) for h in halos]
        scratch += [pltpu.VMEM(current.shape, BF16)]
    else:
        out_shape = [packed, packed]
        scratch += [pltpu.VMEM((3, GROUP * nodes, width), BF16)] + gram_scratch(width)
    return pl.pallas_call(
        functools.partial(product_kernel, sending),
        out_shape=[spread(current.shape, F32)] + out_shape,
        in_specs=[SMEM] * 4 + [VMEM] * (7 if sending else 8),
        out_specs=[VMEM] * (1 + len(out_shape)),
        scratch_shapes=scratch,
        compiler_params=params(28),
        name="product",
    )(columns, sends, count, core, scale, current, blocks, *halos, *([] if sending else [other]))


def gram_scratch(width):
    return [pltpu.VMEM((width, 2 * width), F32), pltpu.VMEM((width, width), F32)]


def gram(count, image):
    width = image.shape[2]
    return pl.pallas_call(
        gram_kernel,
        out_shape=spread((3 * width // 4, width), F32),
        in_specs=[SMEM, VMEM],
        out_specs=VMEM,
        scratch_shapes=gram_scratch(width),
        compiler_params=params(16),
        cost_estimate=pl.CostEstimate(flops=2 * image.size * width, bytes_accessed=image.size * 4, transcendentals=0),
        name="gram",
    )(count, image)


def factor(packed, denominator):
    width = packed.shape[1]
    return pl.pallas_call(
        functools.partial(factor_kernel, denominator),
        out_shape=spread((width, 2 * width), F32),
        in_specs=[VMEM],
        out_specs=VMEM,
        compiler_params=params(16),
        name="factor",
    )(packed)


def last(core, mine, yours, image):
    slots, nodes, width = image.shape
    return pl.pallas_call(
        last_kernel,
        out_shape=[spread(image.shape, F32), spread((width, width), F32)],
        in_specs=[SMEM, VMEM, VMEM, VMEM],
        out_specs=[ANY, VMEM],
        scratch_shapes=[
            pltpu.VMEM((2 * width, 2 * width), BF16),
            pltpu.VMEM(image.shape, F32),
            pltpu.SemaphoreType.DMA((2,)),
        ],
        compiler_params=params(16),
        name="last",
    )(core, mine, yours, image)


def shift(shard, axis, by, wrap):
    size = lax.axis_size(axis)
    route = [(i, (i + by) % size) for i in range(size) if wrap or 0 <= i + by < size]
    return lax.ppermute(shard, axis, route)


def exchange(sent):
    to_next, to_prev, to_right, to_left = sent
    return (shift(to_next, "group", 1, True), shift(to_prev, "group", -1, True),
            shift(to_right, "dom", 1, False), shift(to_left, "dom", -1, False))


def place():
    groups, parts = lax.axis_size("group"), lax.axis_size("dom")
    y = min(groups, 4)
    return groups // y, y, parts // 2, 2


def neighbours(value, dim, by):
    extents = place()
    size = math.prod(extents)
    stride = math.prod(extents[dim + 1:])
    route = []
    for i in range(size):
        at = i // stride % extents[dim]
        route.append((i, i + ((at + by) % extents[dim] - at) * stride))
    return lax.ppermute(value, AXES, route)


def sum_ring(value, dim):
    extent = place()[dim]
    order = sorted(range(1, extent), key=lambda k: min(k, extent - k))
    for piece in [neighbours(value, dim, k) for k in order]:
        value = value + piece
    return value


def sum_far(value):
    extents = place()
    depth, stride = extents[0], math.prod(extents[1:])
    if depth == 1:
        return value
    groups = [[z * stride + i for z in range(depth)] for i in range(stride)]
    copies = jnp.broadcast_to(value, (depth,) + value.shape)
    return lax.all_to_all(copies, AXES, 0, 0, axis_index_groups=groups, tiled=True).sum(0)


def summed(mine, yours):
    value = mine + neighbours(yours, 3, 1)
    value = sum_ring(value, 2)
    value = sum_ring(value, 1)
    return sum_far(value)


def body(blocks, columns, sends, active_row_count, degree, start):
    slots, _, nodes, _ = blocks.shape
    denominator = lax.axis_size("group") * lax.axis_size("dom") * slots * nodes
    sizes = (slots // 2, slots // 2, slots // 4, slots // 4)
    core = lax.rem(lax.axis_index("dom"), 2).reshape(1)
    table = (columns.T, sends, active_row_count, core)
    halo = exchange(prep(sends, degree, start, sizes))
    held, scale = hold(blocks, degree, slots, nodes)
    image, *sent = product(*table, scale, start, held, halo, None)
    halo = exchange(sent)
    first_gram = gram(active_row_count, image)
    image, mine, yours = product(*table, scale, image, held, halo, first_gram)
    work = factor(summed(mine, yours), denominator)
    return tuple(last(core, work, neighbours(work, 3, 1), image))


def solution(mesh):
    return jax.shard_map(
        body,
        mesh=mesh,
        in_specs=(
            P(AXES, None, None, None),
            P(AXES, None),
            P(AXES),
            P(AXES),
            P(AXES, None),
            P(AXES, None, None),
        ),
        out_specs=(P(AXES, None, None), P()),
        check_vma=False,
    )
```

```python
import functools
import math
import jax
import jax.numpy as jnp
from jax import lax
from jax.experimental import pallas as pl
from jax.experimental.pallas import tpu as pltpu
from jax.sharding import PartitionSpec as P

AXES = ("group", "dom")
F32, BF16 = jnp.float32, jnp.bfloat16
PANEL, SUB, GROUP = 16, 8, 13
ANY = pl.BlockSpec(memory_space=pl.ANY)
SMEM = pl.BlockSpec(memory_space=pltpu.SMEM)
VMEM = pl.BlockSpec(memory_space=pltpu.VMEM)


def split3(x):
    high = x.astype(BF16)
    rest = x - high.astype(F32)
    mid = rest.astype(BF16)
    low = (rest - mid.astype(F32)).astype(BF16)
    return high, mid, low


def dot(a, b):
    return jnp.dot(a, b, preferred_element_type=F32)


def dot_rows(a, b):
    return lax.dot_general(a, b, (((0,), (0,)), ((), ())), preferred_element_type=F32)


def scale_blocks(degree_ref):
    scale = lax.rsqrt(degree_ref[...])
    slots, nodes = scale.shape
    turned = jnp.concatenate([scale, jnp.zeros((nodes - slots, nodes), F32)], axis=0).T
    return [jnp.broadcast_to(turned[:, s:s + 1], (nodes, nodes)) for s in range(slots)]


def add_gram(parts, wide_ref, side_ref):
    high, mid, low = parts
    wide_ref[...] += dot_rows(high, jnp.concatenate([high, mid], axis=1))
    left = jnp.concatenate([high, mid * BF16(0.5)], axis=0)
    side_ref[...] += dot_rows(left, jnp.concatenate([low, mid], axis=0))


def finish_gram(wide_ref, side_ref):
    width = side_ref.shape[0]
    cross = wide_ref[:, width:] + side_ref[...]
    return wide_ref[:, :width] + (cross + cross.T)


def pack_gram(gram):
    half, quarter = gram.shape[0] // 2, gram.shape[0] // 4
    left = lax.broadcasted_iota(jnp.int32, (half, gram.shape[1]), 1) < half
    low = gram[half:]
    blocks = jnp.where(left, gram[:half], low)
    corner = jnp.where(left[:quarter], low[:quarter], pltpu.roll(low[quarter:], half, 1))
    return jnp.concatenate([blocks, corner], axis=0)


def unpack_gram(packed):
    size = packed.shape[1]
    half = size // 2
    left = lax.broadcasted_iota(jnp.int32, (half, size), 1) < half
    corner = jnp.concatenate([packed[half:], pltpu.roll(packed[half:], half, 1)], axis=0)
    low = jnp.where(left, corner, packed[:half])
    full = jnp.concatenate([packed[:half], low], axis=0)
    rows = lax.broadcasted_iota(jnp.int32, (size, size), 0)
    columns = lax.broadcasted_iota(jnp.int32, (size, size), 1)
    return jnp.where(rows > columns, full, 0.0) + jnp.where(rows >= columns, full, 0.0).T


def put_sends(out_refs, sends_ref, block_ref):
    base = 0
    for out_ref in out_refs:
        for j in range(out_ref.shape[0]):
            out_ref[j] = block_ref[sends_ref[base + j]]
        base += out_ref.shape[0]


def prep_kernel(sends_hbm, degree_hbm, start_hbm, *refs):
    out_refs = refs[:4]
    operand_ref, sends_ref, degree_ref, start_ref, sems = refs[4:]
    half = start_ref.shape[0] // 2
    halves = [pl.ds(0, half), pl.ds(half, half)]
    copies = [pltpu.make_async_copy(degree_hbm, degree_ref, sems.at[0])]
    copies += [pltpu.make_async_copy(start_hbm.at[part], start_ref.at[part], sems.at[1 + i])
               for i, part in enumerate(halves)]
    copies += [pltpu.make_async_copy(sends_hbm, sends_ref, sems.at[3])]
    for copy in copies:
        copy.start()
    copies[0].wait()
    for s, scale in enumerate(scale_blocks(degree_ref)):
        if s % half == 0:
            copies[1 + s // half].wait()
        operand_ref[s] = (scale * start_ref[s]).astype(BF16)
    copies[3].wait()
    put_sends(out_refs, sends_ref, operand_ref)


def hold_kernel(blocks_hbm, degree_ref, blocks_ref, scale_ref, sem):
    copy = pltpu.make_async_copy(blocks_hbm, blocks_ref, sem)
    copy.start()
    for s, scale in enumerate(scale_blocks(degree_ref)):
        scale_ref[s] = scale
    copy.wait()


def product_kernel(sending, columns_ref, sends_ref, count_ref, core_ref, scale_ref, current_ref,
                   blocks_ref, halo0, halo1, halo2, halo3, *refs):
    if sending:
        image_ref, *out_refs, ext_ref, next_ref = refs
    else:
        other_ref, image_ref, mine_ref, yours_ref, ext_ref, wide_ref, side_ref = refs
    slots, per_row = blocks_ref.shape[:2]
    count = count_ref[0]
    for s in range(slots):
        ext_ref[s] = (scale_ref[s] * current_ref[s]).astype(BF16)
    base = slots
    for piece in (halo0, halo1, halo2, halo3):
        size = piece.shape[0]
        ext_ref[base:base + size] = piece[...]
        base += size
    if not sending:
        wide_ref[...] = jnp.zeros_like(wide_ref)
        side_ref[...] = jnp.zeros_like(side_ref)

    def row(s):
        left = jnp.concatenate([blocks_ref[s, k] for k in range(per_row)], axis=1)
        right = jnp.concatenate([ext_ref[columns_ref[k, s]] for k in range(per_row)], axis=0)
        image = current_ref[s] + scale_ref[s] * dot(left, right)
        return jnp.where(s < count, image, 0.0)

    def rows(step, carry):
        first = step * GROUP
        images = [row(first + i) for i in range(GROUP)]
        for i, image in enumerate(images):
            image_ref[first + i] = image
            if sending:
                next_ref[first + i] = (scale_ref[first + i] * image).astype(BF16)
        if not sending:
            add_gram(split3(jnp.concatenate(images, axis=0)), wide_ref, side_ref)
        return carry
    steps = (count + GROUP - 1) // GROUP
    lax.fori_loop(0, steps, rows, 0)

    def dead(s, carry):
        image_ref[s] = jnp.zeros(image_ref.shape[1:], F32)
        return carry
    lax.fori_loop(steps * GROUP, slots, dead, 0)
    if sending:
        put_sends(out_refs, sends_ref, next_ref)
    else:
        gram = pack_gram(finish_gram(wide_ref, side_ref))
        other, low_core = other_ref[...], core_ref[0] == 0
        mine_ref[...] = jnp.where(low_core, other, gram)
        yours_ref[...] = jnp.where(low_core, gram, other)


def gram_kernel(count_ref, image_ref, gram_ref, wide_ref, side_ref):
    wide_ref[...] = jnp.zeros_like(wide_ref)
    side_ref[...] = jnp.zeros_like(side_ref)

    def rows(step, carry):
        images = [image_ref[step * GROUP + i] for i in range(GROUP)]
        add_gram(split3(jnp.concatenate(images, axis=0)), wide_ref, side_ref)
        return carry
    lax.fori_loop(0, (count_ref[0] + GROUP - 1) // GROUP, rows, 0)
    gram_ref[...] = pack_gram(finish_gram(wide_ref, side_ref))


def gather_rows(rows, sublane):
    lanes = sublane.shape[0]
    pieces = []
    for first in range(0, len(rows), lanes):
        piece = rows[first]
        for j in range(1, lanes):
            piece = jnp.where(sublane == j, rows[first + j], piece)
        pieces.append(piece)
    return jnp.concatenate(pieces, axis=0)


def pair_step(entry, main, side, j, part):
    a, b = entry[j, j], entry[j, j + 1]
    det = a * entry[j + 1, j + 1] - b * b
    first = lax.rsqrt(a)
    second = first * lax.rsqrt(det)
    later = [k for k in part if k > j + 1]
    one = {k: entry[j, k] * first for k in later}
    two = {k: (a * entry[j + 1, k] - b * entry[j, k]) * second for k in later}
    for i in later:
        for k in later:
            if k >= i:
                entry[i, k] = entry[i, k] - one[i] * one[k] - two[i] * two[k]
    for rows in (main, side):
        rows[j + 1] = (a * rows[j + 1] - b * rows[j]) * second
        rows[j] = rows[j] * first
        for i in later:
            rows[i] = rows[i] - one[i] * rows[j] - two[i] * rows[j + 1]


def factorize(work_ref):
    size = work_ref.shape[0]
    step, lanes = PANEL, 8
    sublane = lax.broadcasted_iota(jnp.int32, (lanes, size), 0)
    for top in range(0, size, step):
        rows = work_ref[top:top + step, :]
        main = [jnp.broadcast_to(rows[i:i + 1, :size], (lanes, size)) for i in range(step)]
        side = [jnp.broadcast_to(rows[i:i + 1, size:], (lanes, size)) for i in range(step)]
        for begin in range(0, step, SUB):
            part = range(begin, begin + SUB)
            entry = {(i, k): jnp.broadcast_to(main[i][:, top + k:top + k + 1], (lanes, size))
                     for i in part for k in part if k >= i}
            for j in part[::2]:
                pair_step(entry, main, side, j, part)
            for i in range(begin + SUB, step):
                for j in part:
                    factor = jnp.broadcast_to(main[j][:, top + i:top + i + 1], (lanes, size))
                    main[i] = main[i] - factor * main[j]
                    side[i] = side[i] - factor * side[j]
        both = jnp.concatenate([gather_rows(main, sublane), gather_rows(side, sublane)], axis=1)
        work_ref[top:top + step, :] = both
        if top + step < size:
            h, m, l = split3(both)
            a, b, c = h[:, :size], m[:, :size], l[:, :size]
            left = jnp.concatenate([a, a, b, b, a, c], axis=0)
            right = jnp.concatenate([h, m, h, m, l, h], axis=0)
            turned, near = left.T, top + step
            work_ref[near:near + step, :] -= dot(turned[near:near + step], right)
            if near + step < size:
                work_ref[near + step:, :] -= dot(turned[near + step:], right)


def start_factor(gram, work_ref):
    size = work_ref.shape[0]
    same = (lax.broadcasted_iota(jnp.int32, (size, size), 0)
            == lax.broadcasted_iota(jnp.int32, (size, size), 1))
    diagonal = jnp.where(same, gram, 0.0)
    across = jnp.sum(diagonal, axis=0, keepdims=True)
    down = jnp.sum(diagonal, axis=1, keepdims=True)
    inverse_root = lax.rsqrt(across)
    work_ref[:, :size] = gram * lax.rsqrt(down) * inverse_root
    work_ref[:, size:] = jnp.where(same, inverse_root, 0.0)
    factorize(work_ref)
    return across * inverse_root


def dot_full(a, b):
    ah, am, al = split3(a)
    bh, bm, bl = split3(b)
    left = jnp.concatenate([ah, ah, am, ah, am, al], axis=1)
    right = jnp.concatenate([bh, bm, bh, bl, bm, bh], axis=0)
    return dot(left, right)


def wide_weights(weights, wide_ref):
    high, mid, _ = split3(weights)
    half = jnp.concatenate([high, mid], axis=1)
    wide_ref[...] = jnp.concatenate([half, half], axis=0)


def times_weights(image, wide_ref):
    width = image.shape[1]
    high = image.astype(BF16)
    mid = (image - high.astype(F32)).astype(BF16)
    both = dot(jnp.concatenate([high, mid], axis=1), wide_ref[...])
    return both[:, :width] + both[:, width:]


def factor_kernel(denominator, gram_ref, work_ref):
    root = start_factor(unpack_gram(gram_ref[...]) * F32(1.0 / denominator), work_ref)
    work_ref[:, :work_ref.shape[0]] *= root


def last_kernel(core_ref, mine_ref, yours_ref, image_ref, basis_hbm, factor_ref,
                weights_ref, basis_ref, out_sems):
    slots, nodes, width = image_ref.shape
    low_core = core_ref[0] == 0
    both = jnp.where(low_core, yours_ref[...], mine_ref[...])
    first = jnp.where(low_core, mine_ref[:, width:], yours_ref[:, width:])
    wide_weights(both[:, width:].T, weights_ref)
    half = slots // 2

    def out_copy(part):
        chunk = pl.ds(part * half, half)
        return pltpu.make_async_copy(basis_ref.at[chunk], basis_hbm.at[chunk], out_sems.at[part])

    def apply(s, carry):
        basis_ref[s] = times_weights(image_ref[s], weights_ref)
        return carry
    for part in range(2):
        lax.fori_loop(part * half, (part + 1) * half, apply, 0, unroll=half)
        out_copy(part).start()
    rows = lax.broadcasted_iota(jnp.int32, (width, width), 0)
    columns = lax.broadcasted_iota(jnp.int32, (width, width), 1)
    joint = jnp.where(rows <= columns, both[:, :width], 0.0).T
    factor_ref[...] = jnp.where(rows >= columns, dot_full(first, joint), 0.0)
    for part in range(2):
        out_copy(part).wait()


def params(limit):
    return pltpu.CompilerParams(vmem_limit_bytes=limit * 2**20)


def spread(shape, dtype):
    return jax.ShapeDtypeStruct(shape, dtype)


def prep(sends, degree, start, sizes):
    slots, nodes, width = start.shape
    return pl.pallas_call(
        prep_kernel,
        out_shape=[spread((n, nodes, width), BF16) for n in sizes],
        in_specs=[ANY] * 3,
        out_specs=[VMEM] * 4,
        scratch_shapes=[
            pltpu.VMEM(start.shape, BF16),
            pltpu.SMEM(sends.shape, sends.dtype),
            pltpu.VMEM(degree.shape, F32),
            pltpu.VMEM(start.shape, F32),
            pltpu.SemaphoreType.DMA((4,)),
        ],
        compiler_params=params(58),
        name="prep",
    )(sends, degree, start)


def hold(blocks, degree, slots, nodes):
    size = blocks.size * blocks.dtype.itemsize
    return pl.pallas_call(
        hold_kernel,
        out_shape=[spread(blocks.shape, BF16), spread((slots, nodes, nodes), F32)],
        in_specs=[ANY, VMEM],
        out_specs=[VMEM, VMEM],
        scratch_shapes=[pltpu.SemaphoreType.DMA(())],
        compiler_params=params(36),
        cost_estimate=pl.CostEstimate(flops=0, bytes_accessed=2 * size, transcendentals=0),
        name="hold",
    )(blocks, degree)


def product(columns, sends, count, core, scale, current, blocks, halos, other):
    slots, nodes, width = current.shape
    sizes = [h.shape[0] for h in halos]
    sending = other is None
    packed = spread((3 * width // 4, width), F32)
    scratch = [pltpu.VMEM((slots + sum(sizes), nodes, width), BF16)]
    if sending:
        out_shape = [spread(h.shape, BF16) for h in halos]
        scratch += [pltpu.VMEM(current.shape, BF16)]
    else:
        out_shape = [packed, packed]
        scratch += gram_scratch(width)
    return pl.pallas_call(
        functools.partial(product_kernel, sending),
        out_shape=[spread(current.shape, F32)] + out_shape,
        in_specs=[SMEM] * 4 + [VMEM] * (7 if sending else 8),
        out_specs=[VMEM] * (1 + len(out_shape)),
        scratch_shapes=scratch,
        compiler_params=params(28),
        name="product",
    )(columns, sends, count, core, scale, current, blocks, *halos, *([] if sending else [other]))


def gram_scratch(width):
    return [pltpu.VMEM((width, 2 * width), F32), pltpu.VMEM((width, width), F32)]


def gram(count, image):
    width = image.shape[2]
    return pl.pallas_call(
        gram_kernel,
        out_shape=spread((3 * width // 4, width), F32),
        in_specs=[SMEM, VMEM],
        out_specs=VMEM,
        scratch_shapes=gram_scratch(width),
        compiler_params=params(16),
        cost_estimate=pl.CostEstimate(flops=2 * image.size * width, bytes_accessed=image.size * 4, transcendentals=0),
        name="gram",
    )(count, image)


def factor(packed, denominator):
    width = packed.shape[1]
    return pl.pallas_call(
        functools.partial(factor_kernel, denominator),
        out_shape=spread((width, 2 * width), F32),
        in_specs=[VMEM],
        out_specs=VMEM,
        compiler_params=params(16),
        name="factor",
    )(packed)


def last(core, mine, yours, image):
    slots, nodes, width = image.shape
    return pl.pallas_call(
        last_kernel,
        out_shape=[spread(image.shape, F32), spread((width, width), F32)],
        in_specs=[SMEM, VMEM, VMEM, VMEM],
        out_specs=[ANY, VMEM],
        scratch_shapes=[
            pltpu.VMEM((2 * width, 2 * width), BF16),
            pltpu.VMEM(image.shape, F32),
            pltpu.SemaphoreType.DMA((2,)),
        ],
        compiler_params=params(16),
        name="last",
    )(core, mine, yours, image)


def shift(shard, axis, by, wrap):
    size = lax.axis_size(axis)
    route = [(i, (i + by) % size) for i in range(size) if wrap or 0 <= i + by < size]
    return lax.ppermute(shard, axis, route)


def exchange(sent):
    to_next, to_prev, to_right, to_left = sent
    return (shift(to_next, "group", 1, True), shift(to_prev, "group", -1, True),
            shift(to_right, "dom", 1, False), shift(to_left, "dom", -1, False))


def place():
    groups, parts = lax.axis_size("group"), lax.axis_size("dom")
    y = min(groups, 4)
    return groups // y, y, parts // 2, 2


def neighbours(value, dim, by):
    extents = place()
    size = math.prod(extents)
    stride = math.prod(extents[dim + 1:])
    route = []
    for i in range(size):
        at = i // stride % extents[dim]
        route.append((i, i + ((at + by) % extents[dim] - at) * stride))
    return lax.ppermute(value, AXES, route)


def sum_ring(value, dim):
    extent = place()[dim]
    order = sorted(range(1, extent), key=lambda k: min(k, extent - k))
    for piece in [neighbours(value, dim, k) for k in order]:
        value = value + piece
    return value


def sum_far(value):
    extents = place()
    depth, stride = extents[0], math.prod(extents[1:])
    if depth == 1:
        return value
    groups = [[z * stride + i for z in range(depth)] for i in range(stride)]
    copies = jnp.broadcast_to(value, (depth,) + value.shape)
    return lax.all_to_all(copies, AXES, 0, 0, axis_index_groups=groups, tiled=True).sum(0)


def summed(mine, yours):
    value = mine + neighbours(yours, 3, 1)
    value = sum_ring(value, 2)
    value = sum_ring(value, 1)
    return sum_far(value)


def body(blocks, columns, sends, active_row_count, degree, start):
    slots, _, nodes, _ = blocks.shape
    denominator = lax.axis_size("group") * lax.axis_size("dom") * slots * nodes
    sizes = (slots // 2, slots // 2, slots // 4, slots // 4)
    core = lax.rem(lax.axis_index("dom"), 2).reshape(1)
    table = (columns.T, sends, active_row_count, core)
    halo = exchange(prep(sends, degree, start, sizes))
    held, scale = hold(blocks, degree, slots, nodes)
    image, *sent = product(*table, scale, start, held, halo, None)
    halo = exchange(sent)
    first_gram = gram(active_row_count, image)
    image, mine, yours = product(*table, scale, image, held, halo, first_gram)
    work = factor(summed(mine, yours), denominator)
    return tuple(last(core, work, neighbours(work, 3, 1), image))


def solution(mesh):
    return jax.shard_map(
        body,
        mesh=mesh,
        in_specs=(
            P(AXES, None, None, None),
            P(AXES, None),
            P(AXES),
            P(AXES),
            P(AXES, None),
            P(AXES, None, None),
        ),
        out_specs=(P(AXES, None, None), P()),
        check_vma=False,
    )
```

```python
import functools
import math
import jax
import jax.numpy as jnp
from jax import lax
from jax.experimental import pallas as pl
from jax.experimental.pallas import tpu as pltpu
from jax.sharding import PartitionSpec as P

AXES = ("group", "dom")
F32, BF16 = jnp.float32, jnp.bfloat16
PANEL, SUB, GROUP = 16, 8, 13
ANY = pl.BlockSpec(memory_space=pl.ANY)
SMEM = pl.BlockSpec(memory_space=pltpu.SMEM)
VMEM = pl.BlockSpec(memory_space=pltpu.VMEM)


def split3(x):
    high = x.astype(BF16)
    rest = x - high.astype(F32)
    mid = rest.astype(BF16)
    low = (rest - mid.astype(F32)).astype(BF16)
    return high, mid, low


def dot(a, b):
    return jnp.dot(a, b, preferred_element_type=F32)


def dot_rows(a, b):
    return lax.dot_general(a, b, (((0,), (0,)), ((), ())), preferred_element_type=F32)


def scale_blocks(degree_ref):
    scale = lax.rsqrt(degree_ref[...])
    slots, nodes = scale.shape
    turned = jnp.concatenate([scale, jnp.zeros((nodes - slots, nodes), F32)], axis=0).T
    return [jnp.broadcast_to(turned[:, s:s + 1], (nodes, nodes)) for s in range(slots)]


def add_gram(parts, wide_ref, side_ref):
    high, mid, low = parts
    wide_ref[...] += dot_rows(high, jnp.concatenate([high, mid], axis=1))
    left = jnp.concatenate([high, mid * BF16(0.5)], axis=0)
    side_ref[...] += dot_rows(left, jnp.concatenate([low, mid], axis=0))


def finish_gram(wide_ref, side_ref):
    width = side_ref.shape[0]
    cross = wide_ref[:, width:] + side_ref[...]
    return wide_ref[:, :width] + (cross + cross.T)


def lane_masks(rows, size):
    lane = lax.broadcasted_iota(jnp.int32, (rows, size), 1)
    return lane < size // 2, lane % (size // 2) < size // 4


def pack_gram(gram):
    size = gram.shape[0]
    half, quarter, eighth = size // 2, size // 4, size // 8
    left, first = lane_masks(half, size)
    low = gram[half:]
    blocks = jnp.where(left, gram[:half], low)
    upper, lower = blocks[:quarter], blocks[quarter:]
    diagonal = jnp.where(first[:quarter], upper, lower)
    below = jnp.where(first[:eighth], lower[:eighth], pltpu.roll(lower[eighth:], quarter, 1))
    corner = jnp.where(left[:quarter], low[:quarter], pltpu.roll(low[quarter:], half, 1))
    return jnp.concatenate([diagonal, below, corner], axis=0)


def unpack_gram(packed):
    size = packed.shape[1]
    half, quarter, eighth = size // 2, size // 4, size // 8
    left, first = lane_masks(half, size)
    diagonal, below, corner = packed[:quarter], packed[quarter:quarter + eighth], packed[quarter + eighth:]
    below = jnp.concatenate([below, pltpu.roll(below, size - quarter, 1)], axis=0)
    blocks = jnp.concatenate([diagonal, jnp.where(first[:quarter], below, diagonal)], axis=0)
    corner = jnp.concatenate([corner, pltpu.roll(corner, half, 1)], axis=0)
    full = jnp.concatenate([blocks, jnp.where(left, corner, blocks)], axis=0)
    rows = lax.broadcasted_iota(jnp.int32, (size, size), 0)
    columns = lax.broadcasted_iota(jnp.int32, (size, size), 1)
    return jnp.where(rows > columns, full, 0.0) + jnp.where(rows >= columns, full, 0.0).T


def put_sends(out_refs, sends_ref, block_ref):
    base = 0
    for out_ref in out_refs:
        for j in range(out_ref.shape[0]):
            out_ref[j] = block_ref[sends_ref[base + j]]
        base += out_ref.shape[0]


def prep_kernel(sends_hbm, degree_hbm, start_hbm, *refs):
    out_refs = refs[:4]
    operand_ref, sends_ref, degree_ref, start_ref, sems = refs[4:]
    half = start_ref.shape[0] // 2
    halves = [pl.ds(0, half), pl.ds(half, half)]
    copies = [pltpu.make_async_copy(degree_hbm, degree_ref, sems.at[0])]
    copies += [pltpu.make_async_copy(start_hbm.at[part], start_ref.at[part], sems.at[1 + i])
               for i, part in enumerate(halves)]
    copies += [pltpu.make_async_copy(sends_hbm, sends_ref, sems.at[3])]
    for copy in copies:
        copy.start()
    copies[0].wait()
    for s, scale in enumerate(scale_blocks(degree_ref)):
        if s % half == 0:
            copies[1 + s // half].wait()
        operand_ref[s] = (scale * start_ref[s]).astype(BF16)
    copies[3].wait()
    put_sends(out_refs, sends_ref, operand_ref)


def hold_kernel(blocks_hbm, degree_ref, blocks_ref, scale_ref, sem):
    copy = pltpu.make_async_copy(blocks_hbm, blocks_ref, sem)
    copy.start()
    for s, scale in enumerate(scale_blocks(degree_ref)):
        scale_ref[s] = scale
    copy.wait()


def product_kernel(sending, columns_ref, sends_ref, count_ref, core_ref, scale_ref, current_ref,
                   blocks_ref, halo0, halo1, halo2, halo3, *refs):
    if sending:
        image_ref, *out_refs, ext_ref, next_ref = refs
    else:
        other_ref, image_ref, mine_ref, yours_ref, ext_ref, wide_ref, side_ref = refs
    slots, per_row = blocks_ref.shape[:2]
    count = count_ref[0]
    for s in range(slots):
        ext_ref[s] = (scale_ref[s] * current_ref[s]).astype(BF16)
    base = slots
    for piece in (halo0, halo1, halo2, halo3):
        size = piece.shape[0]
        ext_ref[base:base + size] = piece[...]
        base += size
    if not sending:
        wide_ref[...] = jnp.zeros_like(wide_ref)
        side_ref[...] = jnp.zeros_like(side_ref)

    def row(s):
        left = jnp.concatenate([blocks_ref[s, k] for k in range(per_row)], axis=1)
        right = jnp.concatenate([ext_ref[columns_ref[k, s]] for k in range(per_row)], axis=0)
        image = current_ref[s] + scale_ref[s] * dot(left, right)
        return jnp.where(s < count, image, 0.0)

    def rows(step, carry):
        first = step * GROUP
        images = [row(first + i) for i in range(GROUP)]
        for i, image in enumerate(images):
            image_ref[first + i] = image
            if sending:
                next_ref[first + i] = (scale_ref[first + i] * image).astype(BF16)
        if not sending:
            add_gram(split3(jnp.concatenate(images, axis=0)), wide_ref, side_ref)
        return carry
    steps = (count + GROUP - 1) // GROUP
    lax.fori_loop(0, steps, rows, 0)

    def dead(s, carry):
        image_ref[s] = jnp.zeros(image_ref.shape[1:], F32)
        return carry
    lax.fori_loop(steps * GROUP, slots, dead, 0)
    if sending:
        put_sends(out_refs, sends_ref, next_ref)
    else:
        gram = pack_gram(finish_gram(wide_ref, side_ref))
        other, low_core = other_ref[...], core_ref[0] == 0
        mine_ref[...] = jnp.where(low_core, other, gram)
        yours_ref[...] = jnp.where(low_core, gram, other)


def gram_kernel(count_ref, image_ref, gram_ref, wide_ref, side_ref):
    wide_ref[...] = jnp.zeros_like(wide_ref)
    side_ref[...] = jnp.zeros_like(side_ref)

    def rows(step, carry):
        images = [image_ref[step * GROUP + i] for i in range(GROUP)]
        add_gram(split3(jnp.concatenate(images, axis=0)), wide_ref, side_ref)
        return carry
    lax.fori_loop(0, (count_ref[0] + GROUP - 1) // GROUP, rows, 0)
    gram_ref[...] = pack_gram(finish_gram(wide_ref, side_ref))


def gather_rows(rows, sublane):
    lanes = sublane.shape[0]
    pieces = []
    for first in range(0, len(rows), lanes):
        piece = rows[first]
        for j in range(1, lanes):
            piece = jnp.where(sublane == j, rows[first + j], piece)
        pieces.append(piece)
    return jnp.concatenate(pieces, axis=0)


def pair_step(entry, main, side, j, part):
    a, b = entry[j, j], entry[j, j + 1]
    det = a * entry[j + 1, j + 1] - b * b
    first = lax.rsqrt(a)
    second = first * lax.rsqrt(det)
    later = [k for k in part if k > j + 1]
    one = {k: entry[j, k] * first for k in later}
    two = {k: (a * entry[j + 1, k] - b * entry[j, k]) * second for k in later}
    for i in later:
        for k in later:
            if k >= i:
                entry[i, k] = entry[i, k] - one[i] * one[k] - two[i] * two[k]
    for rows in (main, side):
        rows[j + 1] = (a * rows[j + 1] - b * rows[j]) * second
        rows[j] = rows[j] * first
        for i in later:
            rows[i] = rows[i] - one[i] * rows[j] - two[i] * rows[j + 1]


def factorize(work_ref):
    size = work_ref.shape[0]
    step, lanes = PANEL, 8
    sublane = lax.broadcasted_iota(jnp.int32, (lanes, size), 0)
    for top in range(0, size, step):
        rows = work_ref[top:top + step, :]
        main = [jnp.broadcast_to(rows[i:i + 1, :size], (lanes, size)) for i in range(step)]
        side = [jnp.broadcast_to(rows[i:i + 1, size:], (lanes, size)) for i in range(step)]
        for begin in range(0, step, SUB):
            part = range(begin, begin + SUB)
            entry = {(i, k): jnp.broadcast_to(main[i][:, top + k:top + k + 1], (lanes, size))
                     for i in part for k in part if k >= i}
            for j in part[::2]:
                pair_step(entry, main, side, j, part)
            for i in range(begin + SUB, step):
                for j in part:
                    factor = jnp.broadcast_to(main[j][:, top + i:top + i + 1], (lanes, size))
                    main[i] = main[i] - factor * main[j]
                    side[i] = side[i] - factor * side[j]
        both = jnp.concatenate([gather_rows(main, sublane), gather_rows(side, sublane)], axis=1)
        work_ref[top:top + step, :] = both
        if top + step < size:
            h, m, l = split3(both)
            a, b, c = h[:, :size], m[:, :size], l[:, :size]
            left = jnp.concatenate([a, a, b, b, a, c], axis=0)
            right = jnp.concatenate([h, m, h, m, l, h], axis=0)
            turned, near = left.T, top + step
            work_ref[near:near + step, :] -= dot(turned[near:near + step], right)
            if near + step < size:
                work_ref[near + step:, :] -= dot(turned[near + step:], right)


def start_factor(gram, work_ref):
    size = work_ref.shape[0]
    same = (lax.broadcasted_iota(jnp.int32, (size, size), 0)
            == lax.broadcasted_iota(jnp.int32, (size, size), 1))
    diagonal = jnp.where(same, gram, 0.0)
    across = jnp.sum(diagonal, axis=0, keepdims=True)
    down = jnp.sum(diagonal, axis=1, keepdims=True)
    inverse_root = lax.rsqrt(across)
    work_ref[:, :size] = gram * lax.rsqrt(down) * inverse_root
    work_ref[:, size:] = jnp.where(same, inverse_root, 0.0)
    factorize(work_ref)
    return across * inverse_root


def dot_full(a, b):
    ah, am, al = split3(a)
    bh, bm, bl = split3(b)
    left = jnp.concatenate([ah, ah, am, ah, am, al], axis=1)
    right = jnp.concatenate([bh, bm, bh, bl, bm, bh], axis=0)
    return dot(left, right)


def wide_weights(weights, wide_ref):
    high, mid, _ = split3(weights)
    half = jnp.concatenate([high, mid], axis=1)
    wide_ref[...] = jnp.concatenate([half, half], axis=0)


def times_weights(image, wide_ref):
    width = image.shape[1]
    high = image.astype(BF16)
    mid = (image - high.astype(F32)).astype(BF16)
    both = dot(jnp.concatenate([high, mid], axis=1), wide_ref[...])
    return both[:, :width] + both[:, width:]


def factor_kernel(denominator, gram_ref, work_ref):
    root = start_factor(unpack_gram(gram_ref[...]) * F32(1.0 / denominator), work_ref)
    work_ref[:, :work_ref.shape[0]] *= root


def last_kernel(core_ref, mine_ref, yours_ref, image_ref, basis_hbm, factor_ref,
                weights_ref, basis_ref, out_sems):
    slots, nodes, width = image_ref.shape
    low_core = core_ref[0] == 0
    both = jnp.where(low_core, yours_ref[...], mine_ref[...])
    first = jnp.where(low_core, mine_ref[:, width:], yours_ref[:, width:])
    wide_weights(both[:, width:].T, weights_ref)
    half = slots // 2

    def out_copy(part):
        chunk = pl.ds(part * half, half)
        return pltpu.make_async_copy(basis_ref.at[chunk], basis_hbm.at[chunk], out_sems.at[part])

    def apply(s, carry):
        basis_ref[s] = times_weights(image_ref[s], weights_ref)
        return carry
    for part in range(2):
        lax.fori_loop(part * half, (part + 1) * half, apply, 0, unroll=half)
        out_copy(part).start()
    rows = lax.broadcasted_iota(jnp.int32, (width, width), 0)
    columns = lax.broadcasted_iota(jnp.int32, (width, width), 1)
    joint = jnp.where(rows <= columns, both[:, :width], 0.0).T
    factor_ref[...] = jnp.where(rows >= columns, dot_full(first, joint), 0.0)
    for part in range(2):
        out_copy(part).wait()


def params(limit):
    return pltpu.CompilerParams(vmem_limit_bytes=limit * 2**20)


def spread(shape, dtype):
    return jax.ShapeDtypeStruct(shape, dtype)


def prep(sends, degree, start, sizes):
    slots, nodes, width = start.shape
    return pl.pallas_call(
        prep_kernel,
        out_shape=[spread((n, nodes, width), BF16) for n in sizes],
        in_specs=[ANY] * 3,
        out_specs=[VMEM] * 4,
        scratch_shapes=[
            pltpu.VMEM(start.shape, BF16),
            pltpu.SMEM(sends.shape, sends.dtype),
            pltpu.VMEM(degree.shape, F32),
            pltpu.VMEM(start.shape, F32),
            pltpu.SemaphoreType.DMA((4,)),
        ],
        compiler_params=params(58),
        name="prep",
    )(sends, degree, start)


def hold(blocks, degree, slots, nodes):
    size = blocks.size * blocks.dtype.itemsize
    return pl.pallas_call(
        hold_kernel,
        out_shape=[spread(blocks.shape, BF16), spread((slots, nodes, nodes), F32)],
        in_specs=[ANY, VMEM],
        out_specs=[VMEM, VMEM],
        scratch_shapes=[pltpu.SemaphoreType.DMA(())],
        compiler_params=params(36),
        cost_estimate=pl.CostEstimate(flops=0, bytes_accessed=2 * size, transcendentals=0),
        name="hold",
    )(blocks, degree)


def product(columns, sends, count, core, scale, current, blocks, halos, other):
    slots, nodes, width = current.shape
    sizes = [h.shape[0] for h in halos]
    sending = other is None
    packed = spread((5 * width // 8, width), F32)
    scratch = [pltpu.VMEM((slots + sum(sizes), nodes, width), BF16)]
    if sending:
        out_shape = [spread(h.shape, BF16) for h in halos]
        scratch += [pltpu.VMEM(current.shape, BF16)]
    else:
        out_shape = [packed, packed]
        scratch += gram_scratch(width)
    return pl.pallas_call(
        functools.partial(product_kernel, sending),
        out_shape=[spread(current.shape, F32)] + out_shape,
        in_specs=[SMEM] * 4 + [VMEM] * (7 if sending else 8),
        out_specs=[VMEM] * (1 + len(out_shape)),
        scratch_shapes=scratch,
        compiler_params=params(28),
        name="product",
    )(columns, sends, count, core, scale, current, blocks, *halos, *([] if sending else [other]))


def gram_scratch(width):
    return [pltpu.VMEM((width, 2 * width), F32), pltpu.VMEM((width, width), F32)]


def gram(count, image):
    width = image.shape[2]
    return pl.pallas_call(
        gram_kernel,
        out_shape=spread((5 * width // 8, width), F32),
        in_specs=[SMEM, VMEM],
        out_specs=VMEM,
        scratch_shapes=gram_scratch(width),
        compiler_params=params(16),
        cost_estimate=pl.CostEstimate(flops=2 * image.size * width, bytes_accessed=image.size * 4, transcendentals=0),
        name="gram",
    )(count, image)


def factor(packed, denominator):
    width = packed.shape[1]
    return pl.pallas_call(
        functools.partial(factor_kernel, denominator),
        out_shape=spread((width, 2 * width), F32),
        in_specs=[VMEM],
        out_specs=VMEM,
        compiler_params=params(16),
        name="factor",
    )(packed)


def last(core, mine, yours, image):
    slots, nodes, width = image.shape
    return pl.pallas_call(
        last_kernel,
        out_shape=[spread(image.shape, F32), spread((width, width), F32)],
        in_specs=[SMEM, VMEM, VMEM, VMEM],
        out_specs=[ANY, VMEM],
        scratch_shapes=[
            pltpu.VMEM((2 * width, 2 * width), BF16),
            pltpu.VMEM(image.shape, F32),
            pltpu.SemaphoreType.DMA((2,)),
        ],
        compiler_params=params(16),
        name="last",
    )(core, mine, yours, image)


def shift(shard, axis, by, wrap):
    size = lax.axis_size(axis)
    route = [(i, (i + by) % size) for i in range(size) if wrap or 0 <= i + by < size]
    return lax.ppermute(shard, axis, route)


def exchange(sent):
    to_next, to_prev, to_right, to_left = sent
    return (shift(to_next, "group", 1, True), shift(to_prev, "group", -1, True),
            shift(to_right, "dom", 1, False), shift(to_left, "dom", -1, False))


def place():
    groups, parts = lax.axis_size("group"), lax.axis_size("dom")
    y = min(groups, 4)
    return groups // y, y, parts // 2, 2


def neighbours(value, dim, by):
    extents = place()
    size = math.prod(extents)
    stride = math.prod(extents[dim + 1:])
    route = []
    for i in range(size):
        at = i // stride % extents[dim]
        route.append((i, i + ((at + by) % extents[dim] - at) * stride))
    return lax.ppermute(value, AXES, route)


def sum_ring(value, dim):
    extent = place()[dim]
    order = sorted(range(1, extent), key=lambda k: min(k, extent - k))
    for piece in [neighbours(value, dim, k) for k in order]:
        value = value + piece
    return value


def sum_far(value):
    extents = place()
    depth, stride = extents[0], math.prod(extents[1:])
    if depth == 1:
        return value
    groups = [[z * stride + i for z in range(depth)] for i in range(stride)]
    copies = jnp.broadcast_to(value, (depth,) + value.shape)
    return lax.all_to_all(copies, AXES, 0, 0, axis_index_groups=groups, tiled=True).sum(0)


def summed(mine, yours):
    value = mine + neighbours(yours, 3, 1)
    value = sum_ring(value, 2)
    value = sum_ring(value, 1)
    return sum_far(value)


def body(blocks, columns, sends, active_row_count, degree, start):
    slots, _, nodes, _ = blocks.shape
    denominator = lax.axis_size("group") * lax.axis_size("dom") * slots * nodes
    sizes = (slots // 2, slots // 2, slots // 4, slots // 4)
    core = lax.rem(lax.axis_index("dom"), 2).reshape(1)
    table = (columns.T, sends, active_row_count, core)
    halo = exchange(prep(sends, degree, start, sizes))
    held, scale = hold(blocks, degree, slots, nodes)
    image, *sent = product(*table, scale, start, held, halo, None)
    halo = exchange(sent)
    first_gram = gram(active_row_count, image)
    image, mine, yours = product(*table, scale, image, held, halo, first_gram)
    work = factor(summed(mine, yours), denominator)
    return tuple(last(core, work, neighbours(work, 3, 1), image))


def solution(mesh):
    return jax.shard_map(
        body,
        mesh=mesh,
        in_specs=(
            P(AXES, None, None, None),
            P(AXES, None),
            P(AXES),
            P(AXES),
            P(AXES, None),
            P(AXES, None, None),
        ),
        out_specs=(P(AXES, None, None), P()),
        check_vma=False,
    )
```

```python
import functools
import math
import jax
import jax.numpy as jnp
from jax import lax
from jax.experimental import pallas as pl
from jax.experimental.pallas import tpu as pltpu
from jax.sharding import PartitionSpec as P

AXES = ("group", "dom")
F32, BF16 = jnp.float32, jnp.bfloat16
PANEL, SUB, GROUP = 16, 8, 13
ANY = pl.BlockSpec(memory_space=pl.ANY)
SMEM = pl.BlockSpec(memory_space=pltpu.SMEM)
VMEM = pl.BlockSpec(memory_space=pltpu.VMEM)


def split3(x):
    high = x.astype(BF16)
    rest = x - high.astype(F32)
    mid = rest.astype(BF16)
    low = (rest - mid.astype(F32)).astype(BF16)
    return high, mid, low


def dot(a, b):
    return jnp.dot(a, b, preferred_element_type=F32)


def dot_rows(a, b):
    return lax.dot_general(a, b, (((0,), (0,)), ((), ())), preferred_element_type=F32)


def scale_blocks(degree_ref):
    scale = lax.rsqrt(degree_ref[...])
    slots, nodes = scale.shape
    turned = jnp.concatenate([scale, jnp.zeros((nodes - slots, nodes), F32)], axis=0).T
    return [jnp.broadcast_to(turned[:, s:s + 1], (nodes, nodes)) for s in range(slots)]


def add_gram(parts, wide_ref, side_ref):
    high, mid, low = parts
    wide_ref[...] += dot_rows(high, jnp.concatenate([high, mid], axis=1))
    left = jnp.concatenate([high, mid * BF16(0.5)], axis=0)
    side_ref[...] += dot_rows(left, jnp.concatenate([low, mid], axis=0))


def finish_gram(wide_ref, side_ref):
    width = side_ref.shape[0]
    cross = wide_ref[:, width:] + side_ref[...]
    return wide_ref[:, :width] + (cross + cross.T)


def lane_masks(rows, size):
    lane = lax.broadcasted_iota(jnp.int32, (rows, size), 1)
    return lane < size // 2, lane % (size // 2) < size // 4


def pack_gram(gram):
    size = gram.shape[0]
    half, quarter, eighth = size // 2, size // 4, size // 8
    left, first = lane_masks(half, size)
    low = gram[half:]
    blocks = jnp.where(left, gram[:half], low)
    upper, lower = blocks[:quarter], blocks[quarter:]
    diagonal = jnp.where(first[:quarter], upper, lower)
    below = jnp.where(first[:eighth], lower[:eighth], pltpu.roll(lower[eighth:], quarter, 1))
    corner = jnp.where(left[:quarter], low[:quarter], pltpu.roll(low[quarter:], half, 1))
    return jnp.concatenate([diagonal, below, corner], axis=0)


def unpack_gram(packed):
    size = packed.shape[1]
    half, quarter, eighth = size // 2, size // 4, size // 8
    left, first = lane_masks(half, size)
    diagonal, below, corner = packed[:quarter], packed[quarter:quarter + eighth], packed[quarter + eighth:]
    below = jnp.concatenate([below, pltpu.roll(below, size - quarter, 1)], axis=0)
    blocks = jnp.concatenate([diagonal, jnp.where(first[:quarter], below, diagonal)], axis=0)
    corner = jnp.concatenate([corner, pltpu.roll(corner, half, 1)], axis=0)
    full = jnp.concatenate([blocks, jnp.where(left, corner, blocks)], axis=0)
    rows = lax.broadcasted_iota(jnp.int32, (size, size), 0)
    columns = lax.broadcasted_iota(jnp.int32, (size, size), 1)
    return jnp.where(rows > columns, full, 0.0) + jnp.where(rows >= columns, full, 0.0).T


def put_sends(out_refs, sends_ref, block_ref):
    base = 0
    for out_ref in out_refs:
        for j in range(out_ref.shape[0]):
            out_ref[j] = block_ref[sends_ref[base + j]]
        base += out_ref.shape[0]


def prep_kernel(sends_hbm, degree_hbm, start_hbm, *refs):
    out_refs = refs[:4]
    operand_ref, sends_ref, degree_ref, start_ref, sems = refs[4:]
    half = start_ref.shape[0] // 2
    halves = [pl.ds(0, half), pl.ds(half, half)]
    copies = [pltpu.make_async_copy(degree_hbm, degree_ref, sems.at[0])]
    copies += [pltpu.make_async_copy(start_hbm.at[part], start_ref.at[part], sems.at[1 + i])
               for i, part in enumerate(halves)]
    copies += [pltpu.make_async_copy(sends_hbm, sends_ref, sems.at[3])]
    for copy in copies:
        copy.start()
    copies[0].wait()
    for s, scale in enumerate(scale_blocks(degree_ref)):
        if s % half == 0:
            copies[1 + s // half].wait()
        operand_ref[s] = (scale * start_ref[s]).astype(BF16)
    copies[3].wait()
    put_sends(out_refs, sends_ref, operand_ref)


def hold_kernel(blocks_hbm, degree_ref, blocks_ref, scale_ref, sem):
    copy = pltpu.make_async_copy(blocks_hbm, blocks_ref, sem)
    copy.start()
    for s, scale in enumerate(scale_blocks(degree_ref)):
        scale_ref[s] = scale
    copy.wait()


def product_kernel(sending, columns_ref, sends_ref, count_ref, core_ref, scale_ref, current_ref,
                   blocks_ref, halo0, halo1, halo2, halo3, *refs):
    if sending:
        image_ref, *out_refs, ext_ref, next_ref = refs
    else:
        other_ref, image_ref, mine_ref, yours_ref, ext_ref, wide_ref, side_ref = refs
    slots, per_row = blocks_ref.shape[:2]
    count = count_ref[0]
    for s in range(slots):
        ext_ref[s] = (scale_ref[s] * current_ref[s]).astype(BF16)
    base = slots
    for piece in (halo0, halo1, halo2, halo3):
        size = piece.shape[0]
        ext_ref[base:base + size] = piece[...]
        base += size
    if not sending:
        wide_ref[...] = jnp.zeros_like(wide_ref)
        side_ref[...] = jnp.zeros_like(side_ref)

    def row(s):
        left = jnp.concatenate([blocks_ref[s, k] for k in range(per_row)], axis=1)
        right = jnp.concatenate([ext_ref[columns_ref[k, s]] for k in range(per_row)], axis=0)
        image = current_ref[s] + scale_ref[s] * dot(left, right)
        return jnp.where(s < count, image, 0.0)

    def rows(step, carry):
        first = step * GROUP
        images = [row(first + i) for i in range(GROUP)]
        for i, image in enumerate(images):
            image_ref[first + i] = image
            if sending:
                next_ref[first + i] = (scale_ref[first + i] * image).astype(BF16)
        if not sending:
            add_gram(split3(jnp.concatenate(images, axis=0)), wide_ref, side_ref)
        return carry
    steps = (count + GROUP - 1) // GROUP
    lax.fori_loop(0, steps, rows, 0)

    def dead(s, carry):
        image_ref[s] = jnp.zeros(image_ref.shape[1:], F32)
        return carry
    lax.fori_loop(steps * GROUP, slots, dead, 0)
    if sending:
        put_sends(out_refs, sends_ref, next_ref)
    else:
        gram = pack_gram(finish_gram(wide_ref, side_ref))
        other, low_core = other_ref[...], core_ref[0] == 0
        mine_ref[...] = jnp.where(low_core, other, gram)
        yours_ref[...] = jnp.where(low_core, gram, other)


def gram_kernel(count_ref, image_ref, gram_ref, wide_ref, side_ref):
    wide_ref[...] = jnp.zeros_like(wide_ref)
    side_ref[...] = jnp.zeros_like(side_ref)

    def rows(step, carry):
        images = [image_ref[step * GROUP + i] for i in range(GROUP)]
        add_gram(split3(jnp.concatenate(images, axis=0)), wide_ref, side_ref)
        return carry
    lax.fori_loop(0, (count_ref[0] + GROUP - 1) // GROUP, rows, 0)
    gram_ref[...] = pack_gram(finish_gram(wide_ref, side_ref))


def gather_rows(rows, sublane):
    lanes = sublane.shape[0]
    pieces = []
    for first in range(0, len(rows), lanes):
        piece = rows[first]
        for j in range(1, lanes):
            piece = jnp.where(sublane == j, rows[first + j], piece)
        pieces.append(piece)
    return jnp.concatenate(pieces, axis=0)


def pair_step(entry, main, side, j, part):
    a, b = entry[j, j], entry[j, j + 1]
    det = a * entry[j + 1, j + 1] - b * b
    first = lax.rsqrt(a)
    second = first * lax.rsqrt(det)
    later = [k for k in part if k > j + 1]
    one = {k: entry[j, k] * first for k in later}
    two = {k: (a * entry[j + 1, k] - b * entry[j, k]) * second for k in later}
    for i in later:
        for k in later:
            if k >= i:
                entry[i, k] = entry[i, k] - one[i] * one[k] - two[i] * two[k]
    for rows in (main, side):
        rows[j + 1] = (a * rows[j + 1] - b * rows[j]) * second
        rows[j] = rows[j] * first
        for i in later:
            rows[i] = rows[i] - one[i] * rows[j] - two[i] * rows[j + 1]


def factorize(work_ref):
    size = work_ref.shape[0]
    step, lanes = PANEL, 8
    sublane = lax.broadcasted_iota(jnp.int32, (lanes, size), 0)
    for top in range(0, size, step):
        rows = work_ref[top:top + step, :]
        main = [jnp.broadcast_to(rows[i:i + 1, :size], (lanes, size)) for i in range(step)]
        side = [jnp.broadcast_to(rows[i:i + 1, size:], (lanes, size)) for i in range(step)]
        for begin in range(0, step, SUB):
            part = range(begin, begin + SUB)
            entry = {(i, k): jnp.broadcast_to(main[i][:, top + k:top + k + 1], (lanes, size))
                     for i in part for k in part if k >= i}
            for j in part[::2]:
                pair_step(entry, main, side, j, part)
            for i in range(begin + SUB, step):
                for j in part:
                    factor = jnp.broadcast_to(main[j][:, top + i:top + i + 1], (lanes, size))
                    main[i] = main[i] - factor * main[j]
                    side[i] = side[i] - factor * side[j]
        both = jnp.concatenate([gather_rows(main, sublane), gather_rows(side, sublane)], axis=1)
        work_ref[top:top + step, :] = both
        if top + step < size:
            h, m, l = split3(both)
            a, b, c = h[:, :size], m[:, :size], l[:, :size]
            left = jnp.concatenate([a, a, b, b, a, c], axis=0)
            right = jnp.concatenate([h, m, h, m, l, h], axis=0)
            turned, near = left.T, top + step
            work_ref[near:near + step, :] -= dot(turned[near:near + step], right)
            if near + step < size:
                work_ref[near + step:, :] -= dot(turned[near + step:], right)


def start_factor(gram, work_ref):
    size = work_ref.shape[0]
    same = (lax.broadcasted_iota(jnp.int32, (size, size), 0)
            == lax.broadcasted_iota(jnp.int32, (size, size), 1))
    diagonal = jnp.where(same, gram, 0.0)
    across = jnp.sum(diagonal, axis=0, keepdims=True)
    down = jnp.sum(diagonal, axis=1, keepdims=True)
    inverse_root = lax.rsqrt(across)
    work_ref[:, :size] = gram * lax.rsqrt(down) * inverse_root
    work_ref[:, size:] = jnp.where(same, inverse_root, 0.0)
    factorize(work_ref)
    return across * inverse_root


def dot_full(a, b):
    ah, am, al = split3(a)
    bh, bm, bl = split3(b)
    left = jnp.concatenate([ah, ah, am, ah, am, al], axis=1)
    right = jnp.concatenate([bh, bm, bh, bl, bm, bh], axis=0)
    return dot(left, right)


def wide_weights(weights, wide_ref):
    high, mid, _ = split3(weights)
    half = jnp.concatenate([high, mid], axis=1)
    wide_ref[...] = jnp.concatenate([half, half], axis=0)


def times_weights(image, wide_ref):
    width = image.shape[1]
    high = image.astype(BF16)
    mid = (image - high.astype(F32)).astype(BF16)
    both = dot(jnp.concatenate([high, mid], axis=1), wide_ref[...])
    return both[:, :width] + both[:, width:]


def factor_kernel(denominator, gram_ref, work_ref):
    root = start_factor(unpack_gram(gram_ref[...]) * F32(1.0 / denominator), work_ref)
    work_ref[:, :work_ref.shape[0]] *= root


def last_kernel(core_ref, mine_ref, yours_ref, image_ref, basis_hbm, factor_ref,
                weights_ref, basis_ref, out_sems):
    slots, nodes, width = image_ref.shape
    low_core = core_ref[0] == 0
    both = jnp.where(low_core, yours_ref[...], mine_ref[...])
    first = jnp.where(low_core, mine_ref[:, width:], yours_ref[:, width:])
    wide_weights(both[:, width:].T, weights_ref)
    half = slots // 2

    def out_copy(part):
        chunk = pl.ds(part * half, half)
        return pltpu.make_async_copy(basis_ref.at[chunk], basis_hbm.at[chunk], out_sems.at[part])

    def apply(s, carry):
        basis_ref[s] = times_weights(image_ref[s], weights_ref)
        return carry
    for part in range(2):
        lax.fori_loop(part * half, (part + 1) * half, apply, 0, unroll=half)
        out_copy(part).start()
    rows = lax.broadcasted_iota(jnp.int32, (width, width), 0)
    columns = lax.broadcasted_iota(jnp.int32, (width, width), 1)
    joint = jnp.where(rows <= columns, both[:, :width], 0.0).T
    factor_ref[...] = jnp.where(rows >= columns, dot_full(first, joint), 0.0)
    for part in range(2):
        out_copy(part).wait()


def params(limit):
    return pltpu.CompilerParams(vmem_limit_bytes=limit * 2**20)


def spread(shape, dtype):
    return jax.ShapeDtypeStruct(shape, dtype)


def prep(sends, degree, start, sizes):
    slots, nodes, width = start.shape
    return pl.pallas_call(
        prep_kernel,
        out_shape=[spread((n, nodes, width), BF16) for n in sizes],
        in_specs=[ANY] * 3,
        out_specs=[VMEM] * 4,
        scratch_shapes=[
            pltpu.VMEM(start.shape, BF16),
            pltpu.SMEM(sends.shape, sends.dtype),
            pltpu.VMEM(degree.shape, F32),
            pltpu.VMEM(start.shape, F32),
            pltpu.SemaphoreType.DMA((4,)),
        ],
        compiler_params=params(58),
        name="prep",
    )(sends, degree, start)


def hold(blocks, degree, slots, nodes):
    size = blocks.size * blocks.dtype.itemsize
    return pl.pallas_call(
        hold_kernel,
        out_shape=[spread(blocks.shape, BF16), spread((slots, nodes, nodes), F32)],
        in_specs=[ANY, VMEM],
        out_specs=[VMEM, VMEM],
        scratch_shapes=[pltpu.SemaphoreType.DMA(())],
        compiler_params=params(36),
        cost_estimate=pl.CostEstimate(flops=0, bytes_accessed=2 * size, transcendentals=0),
        name="hold",
    )(blocks, degree)


def product(columns, sends, count, core, scale, current, blocks, halos, other):
    slots, nodes, width = current.shape
    sizes = [h.shape[0] for h in halos]
    sending = other is None
    packed = spread((5 * width // 8, width), F32)
    scratch = [pltpu.VMEM((slots + sum(sizes), nodes, width), BF16)]
    if sending:
        out_shape = [spread(h.shape, BF16) for h in halos]
        scratch += [pltpu.VMEM(current.shape, BF16)]
    else:
        out_shape = [packed, packed]
        scratch += gram_scratch(width)
    return pl.pallas_call(
        functools.partial(product_kernel, sending),
        out_shape=[spread(current.shape, F32)] + out_shape,
        in_specs=[SMEM] * 4 + [VMEM] * (7 if sending else 8),
        out_specs=[VMEM] * (1 + len(out_shape)),
        scratch_shapes=scratch,
        compiler_params=params(28),
        name="product",
    )(columns, sends, count, core, scale, current, blocks, *halos, *([] if sending else [other]))


def gram_scratch(width):
    return [pltpu.VMEM((width, 2 * width), F32), pltpu.VMEM((width, width), F32)]


def gram(count, image):
    width = image.shape[2]
    return pl.pallas_call(
        gram_kernel,
        out_shape=spread((5 * width // 8, width), F32),
        in_specs=[SMEM, VMEM],
        out_specs=VMEM,
        scratch_shapes=gram_scratch(width),
        compiler_params=params(16),
        cost_estimate=pl.CostEstimate(flops=2 * image.size * width, bytes_accessed=image.size * 4, transcendentals=0),
        name="gram",
    )(count, image)


def factor(packed, denominator):
    width = packed.shape[1]
    return pl.pallas_call(
        functools.partial(factor_kernel, denominator),
        out_shape=spread((width, 2 * width), F32),
        in_specs=[VMEM],
        out_specs=VMEM,
        compiler_params=params(16),
        name="factor",
    )(packed)


def last(core, mine, yours, image):
    slots, nodes, width = image.shape
    return pl.pallas_call(
        last_kernel,
        out_shape=[spread(image.shape, F32), spread((width, width), F32)],
        in_specs=[SMEM, VMEM, VMEM, VMEM],
        out_specs=[ANY, VMEM],
        scratch_shapes=[
            pltpu.VMEM((2 * width, 2 * width), BF16),
            pltpu.VMEM(image.shape, F32),
            pltpu.SemaphoreType.DMA((2,)),
        ],
        compiler_params=params(16),
        name="last",
    )(core, mine, yours, image)


def shift(shard, axis, by, wrap):
    size = lax.axis_size(axis)
    route = [(i, (i + by) % size) for i in range(size) if wrap or 0 <= i + by < size]
    return lax.ppermute(shard, axis, route)


def exchange(sent):
    to_next, to_prev, to_right, to_left = sent
    return (shift(to_next, "group", 1, True), shift(to_prev, "group", -1, True),
            shift(to_right, "dom", 1, False), shift(to_left, "dom", -1, False))


def place():
    groups, parts = lax.axis_size("group"), lax.axis_size("dom")
    y = min(groups, 4)
    return groups // y, y, parts // 2, 2


def neighbours(value, dim, by):
    extents = place()
    size = math.prod(extents)
    stride = math.prod(extents[dim + 1:])
    route = []
    for i in range(size):
        at = i // stride % extents[dim]
        route.append((i, i + ((at + by) % extents[dim] - at) * stride))
    return lax.ppermute(value, AXES, route)


def sum_ring(value, dim):
    extent = place()[dim]
    order = sorted(range(1, extent), key=lambda k: min(k, extent - k))
    for piece in [neighbours(value, dim, k) for k in order]:
        value = value + piece
    return value


def sum_far(value):
    depth = place()[0]
    if depth == 1:
        return value
    stride = math.prod(place()[1:])
    value = value + lax.ppermute(value, AXES, [(i, i ^ stride) for i in range(depth * stride)])
    order = sorted(range(2, depth, 2), key=lambda k: min(k, depth - k))
    for piece in [neighbours(value, 0, k) for k in order]:
        value = value + piece
    return value


def summed(mine, yours):
    value = mine + neighbours(yours, 3, 1)
    value = sum_ring(value, 2)
    value = sum_ring(value, 1)
    return sum_far(value)


def body(blocks, columns, sends, active_row_count, degree, start):
    slots, _, nodes, _ = blocks.shape
    denominator = lax.axis_size("group") * lax.axis_size("dom") * slots * nodes
    sizes = (slots // 2, slots // 2, slots // 4, slots // 4)
    core = lax.rem(lax.axis_index("dom"), 2).reshape(1)
    table = (columns.T, sends, active_row_count, core)
    halo = exchange(prep(sends, degree, start, sizes))
    held, scale = hold(blocks, degree, slots, nodes)
    image, *sent = product(*table, scale, start, held, halo, None)
    halo = exchange(sent)
    first_gram = gram(active_row_count, image)
    image, mine, yours = product(*table, scale, image, held, halo, first_gram)
    work = factor(summed(mine, yours), denominator)
    return tuple(last(core, work, neighbours(work, 3, 1), image))


def solution(mesh):
    return jax.shard_map(
        body,
        mesh=mesh,
        in_specs=(
            P(AXES, None, None, None),
            P(AXES, None),
            P(AXES),
            P(AXES),
            P(AXES, None),
            P(AXES, None, None),
        ),
        out_specs=(P(AXES, None, None), P()),
        check_vma=False,
    )
```
